512 devices in a mesh: ens: 16 (over z), grid: 32 (over x, y, core).
Axes of the slice: x: 4, y: 4, z: 16, core: 2. Of those that a mesh axis runs over, the one named last changes fastest.
Arguments:
- hidden_mesh_vectors: bfloat16 [16, 1024, 1024], P('ens', 'grid'), may hold values from -6 to 6
- grid_embed: bfloat16 [16384, 1024], P('grid'), may hold values from -6 to 6
- w_src: bfloat16 [1024, 1024], replicated, may hold values from -0.1875 to 0.1875
- readout_matrix: bfloat16 [99, 1024], replicated, may hold values from -0.1875 to 0.1875
- b_out: float32 [99], replicated, may hold values from -3 to 3
- verifying_reanalysis: float32 [99, 16384], P(None, 'grid'), may hold values from -6 to 6
- var_w: float32 [99], replicated, may hold values from 0.1 to 1
- area_w: float32 [16384], P('grid'), may hold values from 0.25 to 7.5
- edge_src: int32 [49152], P('grid'), may hold values from 0 to 1023, as said below
- edge_dst: int32 [49152], P('grid'), may hold values from 0 to 512, as said below
Outputs:
- mesh_vector_derivative: float32 [16, 1024, 1024], P('ens', 'grid')
- loss: float32 [], replicated
The draws below stay inside these ranges and needn't reach their ends.
Inputs may be any that keep to these rules, and one draw needn't show every extreme that they name: `edge_src`: each slot of shard s that is not empty has a source between (s - 1) * 32 and (s + 2) * 32 - 1; an empty slot has source s * 32. `edge_dst`: the value 512 marks an empty slot; in each shard the non-empty slots come first, at least half of the 1536 slots are non-empty, and some shard has none empty.
All inputs are finite; a program needn't handle non-finite values.
Results may differ from the reference program's by a relative error of at most 0.0074.
Values may be sent and summed in bfloat16 or wider, within the bound.
No kernel may reach another device: no remote copies, remote signals or barrier semaphores. Data moves between devices by JAX's collectives and lax.ppermute only.
A program may use at most 64 MiB of HBM per device.

```python
import math
import jax
import jax.numpy as jnp
from jax import lax

C = 1024
V = 99
PTS_DEV = 512
MN_DEV = 32
EDGE_CAP = 1536
MEMBER_TOTAL = 16
GRID_PTS = 16384
MESH_NODES = 1024
GRID_EDGES = 49152


def edge_tables(key):
    device_pieces = GRID_EDGES // EDGE_CAP
    key_short, random_seed_complete, key_dst, key_off = jax.random.split(key, 4)
    short = jax.random.randint(key_short, (device_pieces,), 0, EDGE_CAP // 2 + 1)
    full_shard = jax.random.randint(random_seed_complete, (), 0, device_pieces)
    shard_ids = jnp.arange(device_pieces, dtype=jnp.int32)
    live = jnp.where(shard_ids == full_shard, EDGE_CAP, EDGE_CAP - short)
    slots = jnp.arange(EDGE_CAP, dtype=jnp.int32)
    used = slots[None, :] < live[:, None]
    dest = jax.random.randint(key_dst, (device_pieces, EDGE_CAP), 0, PTS_DEV)
    dest = jnp.where(used, dest, PTS_DEV)
    realization_offset = jax.random.randint(key_off, (device_pieces, EDGE_CAP), -MN_DEV, 2 * MN_DEV)
    own_first = shard_ids[:, None] * MN_DEV
    source = jnp.clip(own_first + realization_offset, 0, MESH_NODES - 1)
    source = jnp.where(used, source, own_first + 0 * realization_offset)
    return (source.reshape(-1).astype(jnp.int32), dest.reshape(-1).astype(jnp.int32))


def draw_edge_src(key, part):
    source, dest = edge_tables(key)
    return source


def draw_edge_dst(key, part):
    source, dest = edge_tables(key)
    return dest


def draw_hidden_mesh_vectors(key, part):
    key = jax.random.fold_in(key, 11)
    sample_index = (jnp.arange(MEMBER_TOTAL, dtype=jnp.float32) / (MEMBER_TOTAL - 1))[:, None, None]
    rise = 0.5 + sample_index
    base = jnp.clip(jax.random.normal(key, (MEMBER_TOTAL, MESH_NODES, C), jnp.float32), -4.0, 4.0)
    return (base * rise).astype(jnp.bfloat16)


def draw_area_w(key, part):
    key = jax.random.fold_in(key, 12)
    along = jnp.arange(GRID_PTS, dtype=jnp.float32) / (GRID_PTS - 1)
    rise = 1.0 + 2.0 * along
    factor = 4.0 ** jax.random.uniform(key, (GRID_PTS,), jnp.float32, 0.0, 1.0)
    return rise * factor / 4.0


def steps_of(stream_key, extent, cuts, least, high):
    factor_of, own = 1.0, jax.random.fold_in(stream_key, 6)
    for dim, parts in cuts:
        draws = jnp.exp(jax.random.uniform(jax.random.fold_in(own, dim), (parts,), jnp.float32, least / len(cuts), high / len(cuts)))
        factor_of = factor_of * jnp.repeat(draws, extent[dim] // parts).reshape([-1 if axis == dim else 1 for axis in range(len(extent))])
    return factor_of


def gaussian(rng, extent, spread, reach, shards=(), kind=jnp.bfloat16):
    array = spread * jax.random.normal(rng, extent, jnp.float32)
    if shards:
        array = array * steps_of(rng, extent, shards, -0.22, 0.18)
    return jnp.clip(array, -reach, reach).astype(kind)


def setup_inputs(seed: int = 0) -> dict:
    splits = jax.random.split(jax.random.key(seed), 11)
    hidden_mesh_vectors = draw_hidden_mesh_vectors(jax.random.fold_in(splits[10], 71), 0)
    grid_embed = gaussian(splits[1], (GRID_PTS, C), 1.0, 6.0, ((0, 32),))
    w_src = gaussian(splits[2], (C, C), C ** -0.5, 0.1875)
    readout_matrix = gaussian(splits[3], (V, C), C ** -0.5, 0.1875)
    b_out = gaussian(splits[4], (V,), 0.5, 3.0, (), jnp.float32)
    verifying_reanalysis = gaussian(splits[5], (V, GRID_PTS), 1.0, 6.0, ((1, 32),), jnp.float32)
    var_w = jnp.clip(jnp.exp(jax.random.uniform(splits[6], (V,), jnp.float32, math.log(0.1), math.log(1.0))), 0.1, 1.0)
    area_w = draw_area_w(jax.random.fold_in(splits[10], 71), 0)
    edge_src = draw_edge_src(jax.random.fold_in(splits[10], 71), 0)
    edge_dst = draw_edge_dst(jax.random.fold_in(splits[10], 71), 0)
    return {"hidden_mesh_vectors": hidden_mesh_vectors, "grid_embed": grid_embed, "w_src": w_src, "readout_matrix": readout_matrix, "b_out": b_out, "verifying_reanalysis": verifying_reanalysis, "var_w": var_w, "area_w": area_w, "edge_src": edge_src, "edge_dst": edge_dst}


smooth_width = 0.1

def softened_magnitude(dispersion_contribution):
    return jnp.sqrt(dispersion_contribution * dispersion_contribution + smooth_width * smooth_width) - smooth_width

def softened_derivative(dispersion_contribution):
    return dispersion_contribution / jnp.sqrt(dispersion_contribution * dispersion_contribution + smooth_width * smooth_width)

def reference(hidden_mesh_vectors, grid_embed, w_src, readout_matrix, b_out, verifying_reanalysis, var_w, area_w, edge_src, edge_dst):
    shard = jnp.arange(GRID_EDGES, dtype=jnp.int32) // EDGE_CAP
    target_point = jnp.where(edge_dst == PTS_DEV, GRID_PTS, shard * PTS_DEV + edge_dst).astype(jnp.int32)
    embed_ext = jnp.concatenate([grid_embed, jnp.zeros((1, C), grid_embed.dtype)], axis=0)
    edge_embed = embed_ext[target_point].astype(jnp.float32)

    def preact_of(nodes):
        projected = jnp.dot(nodes, w_src, preferred_element_type=jnp.float32).astype(jnp.bfloat16)
        return projected[edge_src].astype(jnp.float32) + edge_embed

    def primal_sweep(nodes):
        preact = preact_of(nodes)
        message = (preact * jax.nn.sigmoid(preact)).astype(jnp.bfloat16)
        summed = jax.ops.segment_sum(message.astype(jnp.float32), target_point, num_segments=GRID_PTS + 1)
        aggregate = summed[:GRID_PTS].astype(jnp.bfloat16)
        return jnp.dot(readout_matrix, aggregate.T, preferred_element_type=jnp.float32) + b_out[:, None]
    predicted_sample_stack = lax.map(primal_sweep, hidden_mesh_vectors)
    scaling_coefficient = var_w[:, None] * area_w[None, :]

    def sample_costs(present_sample):
        dispersion_contribution = present_sample[None] - predicted_sample_stack
        return (lax.optimization_barrier(jnp.sum(softened_magnitude(dispersion_contribution), axis=0)), lax.optimization_barrier(jnp.sum(softened_derivative(dispersion_contribution), axis=0)))
    pair_aggregates, pair_sensitivity_list = lax.map(sample_costs, predicted_sample_stack)
    accuracy_contribution = softened_magnitude(predicted_sample_stack - verifying_reanalysis[None])
    loss = jnp.sum(scaling_coefficient[None] * (accuracy_contribution - pair_aggregates / (2.0 * (MEMBER_TOTAL - 1)))) / (MEMBER_TOTAL * V * GRID_PTS)
    prediction_derivative = (scaling_coefficient[None] * (softened_derivative(predicted_sample_stack - verifying_reanalysis[None]) - pair_sensitivity_list / (MEMBER_TOTAL - 1))).astype(jnp.bfloat16)

    def reverse_sweep(pair):
        nodes, grad_fc = pair
        preact = preact_of(nodes)
        sigmoid_pre = jax.nn.sigmoid(preact)
        grad_agg = jnp.dot(grad_fc.T, readout_matrix, preferred_element_type=jnp.float32).astype(jnp.bfloat16)
        grad_ext = jnp.concatenate([grad_agg, jnp.zeros((1, C), jnp.bfloat16)], axis=0)
        grad_msg = grad_ext[target_point].astype(jnp.float32)
        grad_pre = (grad_msg * sigmoid_pre * (1.0 + preact * (1.0 - sigmoid_pre))).astype(jnp.bfloat16)
        grad_proj = jax.ops.segment_sum(grad_pre.astype(jnp.float32), edge_src, num_segments=MESH_NODES).astype(jnp.bfloat16)
        return jnp.dot(grad_proj, w_src.T, preferred_element_type=jnp.float32)
    mesh_vector_derivative = lax.map(reverse_sweep, (hidden_mesh_vectors, prediction_derivative))
    return (mesh_vector_derivative, loss)
```

```python
import functools

import jax
import jax.numpy as jnp
from jax import lax
from jax.experimental import pallas as pl
from jax.experimental.pallas import tpu as pltpu
from jax.sharding import PartitionSpec as P

smooth_width = 0.1
LANES = 128
CHUNK = 256
TILE = 512
f32 = jnp.float32
bf16 = jnp.bfloat16
VMEM = pl.BlockSpec(memory_space=pltpu.VMEM)
ANYWHERE = pl.BlockSpec(memory_space=pl.ANY)


def grant(kibibytes):
    return pltpu.CompilerParams(vmem_limit_bytes=kibibytes * 2**10)


def started(pairs_of_refs, sems):
    copies = [
        pltpu.make_async_copy(source, target, sems.at[index])
        for index, (source, target) in enumerate(pairs_of_refs)
    ]
    for copy in copies:
        copy.start()
    return copies


def one_hot_rows(ids_ref, blocks, count, offset=0):
    row_of = lax.broadcasted_iota(jnp.int32, (count, LANES), 0) + offset
    return jnp.concatenate(
        [(row_of == ids_ref[j : j + 1, :]).astype(bf16) for j in blocks], axis=1
    )


def window_offset(nodes):
    return (lax.axis_index("grid") - 1) * nodes


def forward_kernel(
    lower_ref,
    upper_ref,
    dst_any,
    src_any,
    own_any,
    readout_any,
    bias_any,
    w_any,
    embed_any,
    forecast_ref,
    slope_any,
    dst_ref,
    src_ref,
    own_ref,
    readout_ref,
    bias_ref,
    w_ref,
    embed_ref,
    readout_pad,
    bias_pad,
    gather_ref,
    scatter_ref,
    sources,
    slope_ref,
    in_sems,
    w_sems,
    embed_sems,
    out_sems,
):
    channels = w_ref.shape[1]
    edges = gather_ref.shape[0]
    points = embed_ref.shape[0]
    variables = readout_ref.shape[0]
    members_nodes = own_ref.shape[0]
    window = 3 * members_nodes
    cuts = [slice(first, first + CHUNK) for first in range(0, channels, CHUNK)]
    small = started(
        [
            (dst_any, dst_ref),
            (src_any, src_ref),
            (own_any, own_ref),
            (readout_any, readout_ref),
            (bias_any, bias_ref),
        ],
        in_sems,
    )
    embeds = started([(embed_any.at[:, cut], embed_ref.at[:, cut]) for cut in cuts], embed_sems)
    weights = started([(w_any.at[:, cut], w_ref.at[:, cut]) for cut in cuts], w_sems)
    readout_pad[...] = jnp.zeros_like(readout_pad)
    bias_pad[...] = jnp.zeros_like(bias_pad)
    for slot in range(2):
        sources[slot, points + window :, :] = jnp.zeros((LANES - window, CHUNK), bf16)
    for copy in small:
        copy.wait()
    readout_pad[:variables, :] = readout_ref[...]
    bias_pad[:, :variables] = bias_ref[...]
    nodes = jnp.concatenate([lower_ref[...], own_ref[...], upper_ref[...]], axis=0)
    lane = lax.broadcasted_iota(jnp.int32, (LANES, LANES), 1)

    def build_tables(rows):
        blocks = range(rows.start // LANES, rows.stop // LANES)
        scatter_ref[:, rows] = one_hot_rows(dst_ref, blocks, points)
        for j in blocks:
            block = slice(j * LANES, (j + 1) * LANES)
            point = jnp.broadcast_to(dst_ref[j : j + 1, :], (LANES, LANES)).T
            node = jnp.broadcast_to(src_ref[j : j + 1, :], (LANES, LANES)).T
            node = node - window_offset(members_nodes)
            for first in range(0, points, LANES):
                gather_ref[block, first : first + LANES] = (lane + first == point).astype(bf16)
            gather_ref[block, points:] = (lane == node).astype(bf16)

    steps = [(n, slice(t, t + TILE)) for n in range(len(cuts)) for t in range(0, edges, TILE)]

    def preact_of(step):
        n, rows = step
        if rows.start == 0:
            embeds[n].wait()
            weights[n].wait()
            proj = jnp.dot(nodes, w_ref[:, cuts[n]], preferred_element_type=f32)
            sources[n % 2, :points, :] = embed_ref[:, cuts[n]]
            sources[n % 2, points : points + window, :] = proj.astype(bf16)
        if n == 0:
            build_tables(rows)
        return jnp.dot(gather_ref[rows, :], sources[n % 2], preferred_element_type=f32)

    stores = []
    total = jnp.broadcast_to(bias_pad[...], forecast_ref.shape)
    following = preact_of(steps[0])
    for index, (n, rows) in enumerate(steps):
        preact = following
        if index + 1 < len(steps):
            following = preact_of(steps[index + 1])
        half = 0.5 * preact
        turn = jnp.tanh(half)
        silu = half + half * turn
        slope_ref[rows, cuts[n]] = (0.5 + 0.5 * turn + silu * (0.5 - 0.5 * turn)).astype(bf16)
        part = jnp.dot(scatter_ref[:, rows], silu.astype(bf16), preferred_element_type=f32)
        summed = part if rows.start == 0 else summed + part
        if rows.stop == edges:
            copy = pltpu.make_async_copy(
                slope_ref.at[:, cuts[n]], slope_any.at[:, cuts[n]], out_sems.at[n]
            )
            copy.start()
            stores.append(copy)
            total = total + lax.dot_general(
                summed.astype(bf16),
                readout_pad[:, cuts[n]],
                (((1,), (1,)), ((), ())),
                preferred_element_type=f32,
            )
    forecast_ref[...] = total
    for copy in stores:
        copy.wait()


def forward(lower, upper, dst, src, own, readout, bias, w_src, embed):
    points, channels = embed.shape
    edges = dst.size
    chunks = channels // CHUNK
    held = [(a.shape, a.dtype) for a in (dst, src, own, readout, bias, w_src, embed)]
    held += [((LANES, channels), bf16), ((1, LANES), f32)]
    held += [((edges, points + LANES), bf16), ((points, edges), bf16)]
    held += [((2, points + LANES, CHUNK), bf16), ((edges, channels), bf16)]
    return pl.pallas_call(
        forward_kernel,
        in_specs=[VMEM] * 2 + [ANYWHERE] * 7,
        out_specs=[VMEM, ANYWHERE],
        out_shape=[
            jax.ShapeDtypeStruct((points, LANES), f32),
            jax.ShapeDtypeStruct((edges, channels), bf16),
        ],
        scratch_shapes=[pltpu.VMEM(shape, kind) for shape, kind in held]
        + [pltpu.SemaphoreType.DMA((count,)) for count in (5, chunks, chunks, chunks)],
        compiler_params=grant(55000),
        cost_estimate=pl.CostEstimate(
            flops=4 * edges * points * channels, bytes_accessed=2**23, transcendentals=edges * channels
        ),
        name="forward",
    )(lower, upper, dst, src, own, readout, bias, w_src, embed)


def pair_kernel(variables, forecasts_ref, target_ref, weight_ref, out_ref, grad_ref):
    members, part, _ = forecasts_ref.shape
    step = 8
    loss = jnp.zeros((step, LANES), f32)
    for first in range(0, part, step):
        rows = slice(first, first + step)
        fc = [forecasts_ref[m, rows, :] for m in range(members)]
        target, weight = target_ref[rows, :], weight_ref[rows, :]
        slopes = [jnp.zeros((step, LANES), f32)] * members
        pair = jnp.zeros((step, LANES), f32)
        for m in range(members):
            for k in range(m + 1, members):
                d = fc[m] - fc[k]
                s = d * d + smooth_width * smooth_width
                q = lax.rsqrt(s)
                pair = pair + (s * q - smooth_width)
                slope = d * q
                slopes[m] = slopes[m] + slope
                slopes[k] = slopes[k] - slope
        skill = jnp.zeros((step, LANES), f32)
        for m in range(members):
            d = fc[m] - target
            s = d * d + smooth_width * smooth_width
            q = lax.rsqrt(s)
            skill = skill + (s * q - smooth_width)
            slopes[m] = weight * (d * q - slopes[m] * (1.0 / (members - 1)))
        loss = loss + weight * (skill - pair * (1.0 / (members - 1)))
        for m in range(members):
            grad_ref[m, rows, :] = slopes[m]
    total = jnp.sum(loss, axis=(0, 1), keepdims=True)
    high = total.astype(bf16).astype(f32)
    middle = (total - high).astype(bf16).astype(f32)
    low = total - high - middle
    lane = lax.broadcasted_iota(jnp.int32, (step, LANES), 1)
    row = lax.broadcasted_iota(jnp.int32, (step, LANES), 0)
    note = jnp.where(lane == variables, high, 0.0)
    note = jnp.where(lane == variables + 1, middle, note)
    note = jnp.where(lane == variables + 2, low, note)
    note = jnp.where(row == 0, note, 0.0)
    spare = lane >= variables
    for m in range(members):
        grad_ref[m, :step, :] = jnp.where(spare, note, grad_ref[m, :step, :])
    out_ref[...] = grad_ref[...].astype(bf16)


def pairs(variables, forecasts, target, weight):
    return pl.pallas_call(
        functools.partial(pair_kernel, variables),
        in_specs=[VMEM] * 3,
        out_specs=VMEM,
        out_shape=jax.ShapeDtypeStruct(forecasts.shape, bf16),
        scratch_shapes=[pltpu.VMEM(forecasts.shape, f32)],
        compiler_params=grant(8192),
        cost_estimate=pl.CostEstimate(flops=2**23, bytes_accessed=2**19, transcendentals=2**19),
        name="pairs",
    )(forecasts, target, weight)


def backward_kernel(
    grad_ref,
    dst_any,
    src_any,
    readout_any,
    slope_any,
    lower_ref,
    own_ref,
    upper_ref,
    dst_ref,
    src_ref,
    readout_ref,
    slope_ref,
    readout_pad,
    in_sems,
    slope_sems,
):
    edges, channels = slope_ref.shape
    points = grad_ref.shape[0]
    nodes = own_ref.shape[0]
    variables = readout_ref.shape[0]
    cuts = [slice(first, first + CHUNK) for first in range(0, channels, CHUNK)]
    small = started(
        [(dst_any, dst_ref), (src_any, src_ref), (readout_any, readout_ref)], in_sems
    )
    loads = started([(slope_any.at[:, cut], slope_ref.at[:, cut]) for cut in cuts], slope_sems)
    readout_pad[...] = jnp.zeros_like(readout_pad)
    for copy in small:
        copy.wait()
    readout_pad[:variables, :] = readout_ref[...]
    blocks = range(edges // LANES)
    scatter = one_hot_rows(dst_ref, blocks, points)
    window_table = one_hot_rows(src_ref, blocks, 3 * nodes, window_offset(nodes))
    edge_grad = jnp.dot(grad_ref[...].T, scatter, preferred_element_type=f32).astype(bf16).T
    for n, cut in enumerate(cuts):
        loads[n].wait()
        grad_pre = []
        for first in range(0, edges, TILE):
            rows = slice(first, first + TILE)
            grad_msg = jnp.dot(edge_grad[rows], readout_pad[:, cut], preferred_element_type=f32)
            grad_msg = grad_msg.astype(bf16).astype(f32)
            grad_pre.append((grad_msg * slope_ref[rows, cut].astype(f32)).astype(bf16))
        grad_pre = jnp.concatenate(grad_pre, axis=0)
        window = jnp.dot(window_table, grad_pre, preferred_element_type=f32)
        lower_ref[:, cut] = window[:nodes]
        own_ref[:, cut] = window[nodes : 2 * nodes]
        upper_ref[:, cut] = window[2 * nodes :]


def backward(grad_points, dst, src, readout, slope, nodes):
    edges, channels = slope.shape
    points = grad_points.shape[0]
    held = [(a.shape, a.dtype) for a in (dst, src, readout, slope)] + [((LANES, channels), bf16)]
    return pl.pallas_call(
        backward_kernel,
        in_specs=[VMEM] + [ANYWHERE] * 4,
        out_specs=[VMEM] * 3,
        out_shape=[jax.ShapeDtypeStruct((nodes, channels), f32)] * 3,
        scratch_shapes=[pltpu.VMEM(shape, kind) for shape, kind in held]
        + [pltpu.SemaphoreType.DMA((3,)), pltpu.SemaphoreType.DMA((channels // CHUNK,))],
        compiler_params=grant(53248),
        cost_estimate=pl.CostEstimate(
            flops=2 * edges * points * channels, bytes_accessed=2**22, transcendentals=0
        ),
        name="backward",
    )(grad_points, dst, src, readout, slope)


def shards(
    hidden_mesh_vectors,
    grid_embed,
    w_src,
    readout_matrix,
    b_out,
    verifying_reanalysis,
    var_w,
    area_w,
    edge_src,
    edge_dst,
):
    nodes_dev = hidden_mesh_vectors.shape[1]
    points_dev = grid_embed.shape[0]
    variables = readout_matrix.shape[0]
    members = lax.axis_size("ens")
    part = points_dev // members
    lane_pad = LANES - variables
    ens_rank = lax.axis_index("ens")
    ends = lax.axis_size("grid") - 1
    upward = [(i, i + 1) for i in range(ends)]
    downward = [(i + 1, i) for i in range(ends)]

    own = hidden_mesh_vectors[0]
    lower = lax.ppermute(own, "grid", upward)
    upper = lax.ppermute(own, "grid", downward)

    src = edge_src.reshape(-1, LANES)
    dst = edge_dst.reshape(-1, LANES)
    var_weight = jnp.pad(var_w, (0, lane_pad))
    area = lax.dynamic_slice_in_dim(area_w, ens_rank * part, part, axis=0)
    target = lax.dynamic_slice_in_dim(verifying_reanalysis, ens_rank * part, part, axis=1)
    target = jnp.pad(target.T, ((0, 0), (0, lane_pad)))
    weight = area[:, None] * var_weight[None, :]

    forecast, slope = forward(
        lower, upper, dst, src, own, readout_matrix, b_out[None, :], w_src, grid_embed
    )
    forecasts = lax.all_to_all(forecast.reshape(members, part, LANES), "ens", 0, 0)
    grad_members = pairs(variables, forecasts, target, weight)
    grad_points = lax.all_to_all(grad_members, "ens", 0, 0)

    shards_grid = lax.axis_size("grid")
    notes = jnp.sum(grad_points[:, 0, variables : variables + 3].astype(f32))
    sums = lax.all_to_all(jnp.full((shards_grid, 8, LANES), notes, f32), "grid", 0, 0)
    loss = jnp.sum(sums[:, 0, 0]) / (members * variables * points_dev * shards_grid)

    below, middle, above = backward(
        grad_points.reshape(points_dev, LANES), dst, src, readout_matrix, slope, nodes_dev
    )
    from_above = lax.ppermute(below, "grid", downward)
    from_below = lax.ppermute(above, "grid", upward)
    grad_proj = (middle + from_above + from_below).astype(bf16)
    grad_nodes = lax.dot_general(
        grad_proj, w_src, (((1,), (1,)), ((), ())), preferred_element_type=f32
    )
    return (grad_nodes[None], loss)


def solution(mesh):
    in_specs = (
        P("ens", "grid", None),
        P("grid", None),
        P(),
        P(),
        P(),
        P(None, "grid"),
        P(),
        P("grid"),
        P("grid"),
        P("grid"),
    )
    out_specs = (P("ens", "grid", None), P())
    return jax.shard_map(shards, mesh=mesh, in_specs=in_specs, out_specs=out_specs, check_vma=False)
```

```python
import functools

import jax
import jax.numpy as jnp
from jax import lax
from jax.experimental import pallas as pl
from jax.experimental.pallas import tpu as pltpu
from jax.sharding import PartitionSpec as P

smooth_width = 0.1
LANES = 128
CHUNK = 512
TILE = 512
CODE_STEPS = 1280.0
CODE_SCALE = 64.0
f32 = jnp.float32
bf16 = jnp.bfloat16
VMEM = pl.BlockSpec(memory_space=pltpu.VMEM)
ANYWHERE = pl.BlockSpec(memory_space=pl.ANY)


def grant(kibibytes):
    return pltpu.CompilerParams(vmem_limit_bytes=kibibytes * 2**10)


def started(pairs_of_refs, sems):
    copies = [
        pltpu.make_async_copy(source, target, sems.at[index])
        for index, (source, target) in enumerate(pairs_of_refs)
    ]
    for copy in copies:
        copy.start()
    return copies


def one_hot_rows(ids_ref, blocks, count, offset=0):
    row_of = lax.broadcasted_iota(jnp.int32, (count, LANES), 0) + offset
    return jnp.concatenate(
        [(row_of == ids_ref[j : j + 1, :]).astype(bf16) for j in blocks], axis=1
    )


def window_offset(nodes):
    return (lax.axis_index("grid") - 1) * nodes


def gather_rows(gather_ref, dst_ref, src_ref, blocks, nodes):
    points = gather_ref.shape[1] - LANES
    lane = lax.broadcasted_iota(jnp.int32, (LANES, LANES), 1)
    for j in blocks:
        block = slice(j * LANES, (j + 1) * LANES)
        point = jnp.broadcast_to(dst_ref[j : j + 1, :], (LANES, LANES)).T
        node = jnp.broadcast_to(src_ref[j : j + 1, :], (LANES, LANES)).T
        node = node - window_offset(nodes)
        for first in range(0, points, LANES):
            gather_ref[block, first : first + LANES] = (lane + first == point).astype(bf16)
        gather_ref[block, points:] = (lane == node).astype(bf16)


def forward_kernel(
    lower_ref,
    upper_ref,
    dst_any,
    src_any,
    own_any,
    readout_any,
    bias_any,
    w_any,
    embed_any,
    forecast_ref,
    proj_ref,
    dst_ref,
    src_ref,
    own_ref,
    readout_ref,
    bias_ref,
    w_ref,
    embed_ref,
    readout_pad,
    bias_pad,
    gather_ref,
    scatter_ref,
    sources,
    in_sems,
    w_sems,
    embed_sems,
):
    channels = w_ref.shape[1]
    edges = gather_ref.shape[0]
    points = embed_ref.shape[0]
    variables = readout_ref.shape[0]
    members_nodes = own_ref.shape[0]
    window = 3 * members_nodes
    cuts = [slice(first, first + CHUNK) for first in range(0, channels, CHUNK)]
    small = started(
        [
            (dst_any, dst_ref),
            (src_any, src_ref),
            (own_any, own_ref),
            (readout_any, readout_ref),
            (bias_any, bias_ref),
        ],
        in_sems,
    )
    embeds = started([(embed_any.at[:, cut], embed_ref.at[:, cut]) for cut in cuts], embed_sems)
    weights = started([(w_any.at[:, cut], w_ref.at[:, cut]) for cut in cuts], w_sems)
    readout_pad[...] = jnp.zeros_like(readout_pad)
    bias_pad[...] = jnp.zeros_like(bias_pad)
    for slot in range(2):
        sources[slot, points + window :, :] = jnp.zeros((LANES - window, CHUNK), bf16)
    for copy in small:
        copy.wait()
    readout_pad[:variables, :] = readout_ref[...]
    bias_pad[:, :variables] = bias_ref[...]
    nodes = jnp.concatenate([lower_ref[...], own_ref[...], upper_ref[...]], axis=0)

    def build_tables(rows):
        blocks = range(rows.start // LANES, rows.stop // LANES)
        scatter_ref[:, rows] = one_hot_rows(dst_ref, blocks, points)
        gather_rows(gather_ref, dst_ref, src_ref, blocks, members_nodes)

    steps = [(n, slice(t, t + TILE)) for n in range(len(cuts)) for t in range(0, edges, TILE)]

    def preact_of(step):
        n, rows = step
        if rows.start == 0:
            embeds[n].wait()
            weights[n].wait()
            proj = jnp.dot(nodes, w_ref[:, cuts[n]], preferred_element_type=f32).astype(bf16)
            proj_ref[:, cuts[n]] = proj
            sources[n % 2, :points, :] = embed_ref[:, cuts[n]]
            sources[n % 2, points : points + window, :] = proj
        if n == 0:
            build_tables(rows)
        return jnp.dot(gather_ref[rows, :], sources[n % 2], preferred_element_type=f32)

    total = jnp.broadcast_to(bias_pad[...], forecast_ref.shape)
    following = preact_of(steps[0])
    for index, (n, rows) in enumerate(steps):
        preact = following
        if index + 1 < len(steps):
            following = preact_of(steps[index + 1])
        half = 0.5 * preact
        turn = jnp.tanh(half)
        silu = half + half * turn
        part = jnp.dot(scatter_ref[:, rows], silu.astype(bf16), preferred_element_type=f32)
        summed = part if rows.start == 0 else summed + part
        if rows.stop == edges:
            total = total + lax.dot_general(
                summed.astype(bf16),
                readout_pad[:, cuts[n]],
                (((1,), (1,)), ((), ())),
                preferred_element_type=f32,
            )
    codes = jnp.floor(jnp.log(1.0 + jnp.abs(total) * CODE_SCALE) * CODE_STEPS + 0.5)
    codes = jnp.where(total < 0.0, -codes, codes)
    forecast_ref[...] = codes.astype(jnp.int32).astype(jnp.int16)


def forward(lower, upper, dst, src, own, readout, bias, w_src, embed):
    points, channels = embed.shape
    edges = dst.size
    chunks = channels // CHUNK
    held = [(a.shape, a.dtype) for a in (dst, src, own, readout, bias, w_src, embed)]
    held += [((LANES, channels), bf16), ((1, LANES), f32)]
    held += [((edges, points + LANES), bf16), ((points, edges), bf16)]
    held += [((2, points + LANES, CHUNK), bf16)]
    return pl.pallas_call(
        forward_kernel,
        in_specs=[VMEM] * 2 + [ANYWHERE] * 7,
        out_specs=[VMEM] * 2,
        out_shape=[
            jax.ShapeDtypeStruct((points, LANES), jnp.int16),
            jax.ShapeDtypeStruct((3 * own.shape[0], channels), bf16),
        ],
        scratch_shapes=[pltpu.VMEM(shape, kind) for shape, kind in held]
        + [pltpu.SemaphoreType.DMA((count,)) for count in (5, chunks, chunks)],
        compiler_params=grant(55350),
        cost_estimate=pl.CostEstimate(
            flops=4 * edges * points * channels, bytes_accessed=2**23, transcendentals=edges * channels
        ),
        name="forward",
    )(lower, upper, dst, src, own, readout, bias, w_src, embed)


def pair_kernel(
    variables,
    codes_ref,
    target_ref,
    weight_ref,
    after_ref,
    out_ref,
    forecasts_ref,
    grad_ref,
):
    del after_ref
    members, part, _ = codes_ref.shape
    step = 8
    for m in range(members):
        codes = codes_ref[m].astype(jnp.int32).astype(f32)
        size = (jnp.exp(jnp.abs(codes) * (1.0 / CODE_STEPS)) - 1.0) * (1.0 / CODE_SCALE)
        forecasts_ref[m] = jnp.where(codes < 0.0, -size, size)
    loss = jnp.zeros((step, LANES), f32)
    for first in range(0, part, step):
        rows = slice(first, first + step)
        fc = [forecasts_ref[m, rows, :] for m in range(members)]
        target, weight = target_ref[rows, :], weight_ref[rows, :]
        slopes = [jnp.zeros((step, LANES), f32)] * members
        pair = jnp.zeros((step, LANES), f32)
        for m in range(members):
            for k in range(m + 1, members):
                d = fc[m] - fc[k]
                s = d * d + smooth_width * smooth_width
                q = lax.rsqrt(s)
                pair = pair + (s * q - smooth_width)
                slope = d * q
                slopes[m] = slopes[m] + slope
                slopes[k] = slopes[k] - slope
        skill = jnp.zeros((step, LANES), f32)
        for m in range(members):
            d = fc[m] - target
            s = d * d + smooth_width * smooth_width
            q = lax.rsqrt(s)
            skill = skill + (s * q - smooth_width)
            slopes[m] = weight * (d * q - slopes[m] * (1.0 / (members - 1)))
        loss = loss + weight * (skill - pair * (1.0 / (members - 1)))
        for m in range(members):
            grad_ref[m, rows, :] = slopes[m]
    total = jnp.sum(loss, axis=(0, 1), keepdims=True)
    high = total.astype(bf16).astype(f32)
    middle = (total - high).astype(bf16).astype(f32)
    low = total - high - middle
    lane = lax.broadcasted_iota(jnp.int32, (step, LANES), 1)
    row = lax.broadcasted_iota(jnp.int32, (step, LANES), 0)
    note = jnp.where(lane == variables, high, 0.0)
    note = jnp.where(lane == variables + 1, middle, note)
    note = jnp.where(lane == variables + 2, low, note)
    note = jnp.where(row == 0, note, 0.0)
    spare = lane >= variables
    for m in range(members):
        grad_ref[m, :step, :] = jnp.where(spare, note, grad_ref[m, :step, :])
    out_ref[...] = grad_ref[...].astype(bf16)


def pairs(variables, forecasts, target, weight, after):
    return pl.pallas_call(
        functools.partial(pair_kernel, variables),
        in_specs=[VMEM] * 3 + [ANYWHERE],
        out_specs=VMEM,
        out_shape=jax.ShapeDtypeStruct(forecasts.shape, bf16),
        scratch_shapes=[pltpu.VMEM(forecasts.shape, f32)] * 2,
        compiler_params=grant(8192),
        cost_estimate=pl.CostEstimate(flops=2**23, bytes_accessed=2**19, transcendentals=2**19),
        name="pairs",
    )(forecasts, target, weight, after)


def slope_kernel(
    proj_ref,
    dst_ref,
    src_ref,
    readout_ref,
    embed_ref,
    slope_any,
    window_ref,
    readout_pad,
    gather_ref,
    sources,
    slope_ref,
    sems,
):
    edges, channels = slope_ref.shape
    points = embed_ref.shape[0]
    window = proj_ref.shape[0]
    blocks = range(edges // LANES)
    nodes = window // 3
    gather_rows(gather_ref, dst_ref, src_ref, blocks, nodes)
    window_ref[...] = one_hot_rows(src_ref, blocks, window, window_offset(nodes))
    readout_pad[...] = jnp.zeros_like(readout_pad)
    readout_pad[: readout_ref.shape[0], :] = readout_ref[...]
    sources[points + window :, :] = jnp.zeros((LANES - window, CHUNK), bf16)
    stores = []
    for n, first_channel in enumerate(range(0, channels, CHUNK)):
        cut = slice(first_channel, first_channel + CHUNK)
        sources[:points, :] = embed_ref[:, cut]
        sources[points : points + window, :] = proj_ref[:, cut]
        for first in range(0, edges, TILE):
            rows = slice(first, first + TILE)
            preact = jnp.dot(gather_ref[rows, :], sources[...], preferred_element_type=f32)
            half = 0.5 * preact
            turn = jnp.tanh(half)
            silu = half + half * turn
            slope = 0.5 + 0.5 * turn + silu * (0.5 - 0.5 * turn)
            slope_ref[rows, cut] = slope.astype(bf16)
        stores += started([(slope_ref.at[:, cut], slope_any.at[:, cut])], sems.at[n : n + 1])
    for copy in stores:
        copy.wait()


def slopes(proj, dst, src, readout, embed):
    points, channels = embed.shape
    edges = dst.size
    return pl.pallas_call(
        slope_kernel,
        in_specs=[VMEM] * 5,
        out_specs=[ANYWHERE, VMEM, VMEM],
        out_shape=[
            jax.ShapeDtypeStruct((edges, channels), bf16),
            jax.ShapeDtypeStruct((proj.shape[0], edges), bf16),
            jax.ShapeDtypeStruct((LANES, channels), bf16),
        ],
        scratch_shapes=[
            pltpu.VMEM((edges, points + LANES), bf16),
            pltpu.VMEM((points + LANES, CHUNK), bf16),
            pltpu.VMEM((edges, channels), bf16),
            pltpu.SemaphoreType.DMA((channels // CHUNK,)),
        ],
        compiler_params=grant(53248),
        cost_estimate=pl.CostEstimate(
            flops=2 * edges * points * channels, bytes_accessed=2**23, transcendentals=edges * channels
        ),
        name="slopes",
    )(proj, dst, src, readout, embed)


def backward_kernel(
    grad_ref,
    dst_ref,
    window_ref,
    readout_ref,
    slope_any,
    lower_ref,
    own_ref,
    upper_ref,
    slope_ref,
    sems,
):
    edges, channels = slope_ref.shape
    nodes = own_ref.shape[0]
    cuts = [slice(first, first + CHUNK) for first in range(0, channels, CHUNK)]
    loads = started([(slope_any.at[:, cut], slope_ref.at[:, cut]) for cut in cuts], sems)
    scatter = one_hot_rows(dst_ref, range(edges // LANES), grad_ref.shape[0])
    edge_grad = jnp.dot(grad_ref[...].T, scatter, preferred_element_type=f32)
    edge_grad = edge_grad.astype(bf16).T
    for n, cut in enumerate(cuts):
        loads[n].wait()
        grad_pre = []
        for first in range(0, edges, TILE):
            rows = slice(first, first + TILE)
            grad_msg = jnp.dot(edge_grad[rows], readout_ref[:, cut], preferred_element_type=f32)
            grad_msg = grad_msg.astype(bf16).astype(f32)
            grad_pre.append((grad_msg * slope_ref[rows, cut].astype(f32)).astype(bf16))
        grad_pre = jnp.concatenate(grad_pre, axis=0)
        window = jnp.dot(window_ref[...], grad_pre, preferred_element_type=f32)
        lower_ref[:, cut] = window[:nodes].astype(bf16)
        own_ref[:, cut] = window[nodes : 2 * nodes]
        upper_ref[:, cut] = window[2 * nodes :].astype(bf16)


def backward(grad_points, dst, window, readout, slope, nodes):
    edges, channels = slope.shape
    points = grad_points.shape[0]
    return pl.pallas_call(
        backward_kernel,
        in_specs=[VMEM] * 4 + [ANYWHERE],
        out_specs=[VMEM] * 3,
        out_shape=[jax.ShapeDtypeStruct((nodes, channels), kind) for kind in (bf16, f32, bf16)],
        scratch_shapes=[
            pltpu.VMEM((edges, channels), bf16),
            pltpu.SemaphoreType.DMA((channels // CHUNK,)),
        ],
        compiler_params=grant(53900),
        cost_estimate=pl.CostEstimate(
            flops=2 * edges * points * channels, bytes_accessed=2**22, transcendentals=0
        ),
        name="backward",
    )(grad_points, dst, window, readout, slope)


def note_kernel(variables, grad_ref, notes_ref):
    rows = grad_ref[:, :16, :].astype(f32)
    lane = lax.broadcasted_iota(jnp.int32, rows.shape, 2)
    row = lax.broadcasted_iota(jnp.int32, rows.shape, 1)
    kept = (row == 0) & (lane >= variables) & (lane < variables + 3)
    total = jnp.sum(jnp.sum(jnp.where(kept, rows, 0.0), axis=0), axis=(0, 1), keepdims=True)
    notes_ref[...] = jnp.broadcast_to(total[None], notes_ref.shape)


def loss_notes(variables, grad_points, copies):
    return pl.pallas_call(
        functools.partial(note_kernel, variables),
        in_specs=[VMEM],
        out_specs=VMEM,
        out_shape=jax.ShapeDtypeStruct((copies, 8, LANES), f32),
        compiler_params=grant(4096),
        name="loss_notes",
    )(grad_points)


def finish_kernel(scale, own_ref, above_ref, below_ref, w_ref, notes_ref, grad_ref, loss_ref):
    total = own_ref[...] + above_ref[...].astype(f32) + below_ref[...].astype(f32)
    grad_ref[...] = lax.dot_general(
        total.astype(bf16), w_ref[...], (((1,), (1,)), ((), ())), preferred_element_type=f32
    )
    loss_ref[...] = jnp.sum(notes_ref[...], axis=0)[:1, :1] * scale


def finish(scale, own, above, below, w_src, notes):
    return pl.pallas_call(
        functools.partial(finish_kernel, scale),
        in_specs=[VMEM] * 5,
        out_specs=[VMEM] * 2,
        out_shape=[
            jax.ShapeDtypeStruct((own.shape[0], w_src.shape[0]), f32),
            jax.ShapeDtypeStruct((1, 1), f32),
        ],
        compiler_params=grant(8192),
        cost_estimate=pl.CostEstimate(flops=2**26, bytes_accessed=2**21, transcendentals=0),
        name="finish",
    )(own, above, below, w_src, notes)


def shards(
    hidden_mesh_vectors,
    grid_embed,
    w_src,
    readout_matrix,
    b_out,
    verifying_reanalysis,
    var_w,
    area_w,
    edge_src,
    edge_dst,
):
    nodes_dev = hidden_mesh_vectors.shape[1]
    points_dev = grid_embed.shape[0]
    variables = readout_matrix.shape[0]
    members = lax.axis_size("ens")
    part = points_dev // members
    lane_pad = LANES - variables
    ens_rank = lax.axis_index("ens")
    ends = lax.axis_size("grid") - 1
    upward = [(i, i + 1) for i in range(ends)]
    downward = [(i + 1, i) for i in range(ends)]

    own = hidden_mesh_vectors[0]
    lower = lax.ppermute(own, "grid", upward)
    upper = lax.ppermute(own, "grid", downward)

    src = edge_src.reshape(-1, LANES)
    dst = edge_dst.reshape(-1, LANES)
    var_weight = jnp.pad(var_w, (0, lane_pad))
    area = lax.dynamic_slice_in_dim(area_w, ens_rank * part, part, axis=0)
    target = lax.dynamic_slice_in_dim(verifying_reanalysis, ens_rank * part, part, axis=1)
    target = jnp.pad(target.T, ((0, 0), (0, lane_pad)))
    weight = area[:, None] * var_weight[None, :]

    forecast, proj = forward(
        lower, upper, dst, src, own, readout_matrix, b_out[None, :], w_src, grid_embed
    )
    forecasts = lax.all_to_all(forecast.reshape(members, part, LANES), "ens", 0, 0)
    slope, window, readout = slopes(proj, dst, src, readout_matrix, grid_embed)
    grad_members = pairs(variables, forecasts, target, weight, window)
    grad_points = lax.all_to_all(grad_members, "ens", 0, 0)

    shards_grid = lax.axis_size("grid")
    notes = loss_notes(variables, grad_points, shards_grid)
    notes = lax.all_to_all(notes, "grid", 0, 0)
    below, middle, above = backward(
        grad_points.reshape(points_dev, LANES), dst, window, readout, slope, nodes_dev
    )
    from_above = lax.ppermute(below, "grid", downward)
    from_below = lax.ppermute(above, "grid", upward)
    scale = 1.0 / (members * variables * points_dev * shards_grid)
    grad_nodes, loss = finish(scale, middle, from_above, from_below, w_src, notes)
    return (grad_nodes[None], loss[0, 0])


def solution(mesh):
    in_specs = (
        P("ens", "grid", None),
        P("grid", None),
        P(),
        P(),
        P(),
        P(None, "grid"),
        P(),
        P("grid"),
        P("grid"),
        P("grid"),
    )
    out_specs = (P("ens", "grid", None), P())
    return jax.shard_map(shards, mesh=mesh, in_specs=in_specs, out_specs=out_specs, check_vma=False)
```

```python
import functools

import jax
import jax.numpy as jnp
from jax import lax
from jax.experimental import pallas as pl
from jax.experimental.pallas import tpu as pltpu
from jax.sharding import PartitionSpec as P

smooth_width = 0.1
LANES = 128
CHUNK = 512
TILE = 512
CODE_STEPS = 1280.0
CODE_SCALE = 64.0
f32 = jnp.float32
bf16 = jnp.bfloat16
VMEM = pl.BlockSpec(memory_space=pltpu.VMEM)
ANYWHERE = pl.BlockSpec(memory_space=pl.ANY)


def grant(kibibytes):
    return pltpu.CompilerParams(vmem_limit_bytes=kibibytes * 2**10)


def started(pairs_of_refs, sems):
    copies = [
        pltpu.make_async_copy(source, target, sems.at[index])
        for index, (source, target) in enumerate(pairs_of_refs)
    ]
    for copy in copies:
        copy.start()
    return copies


def one_hot_rows(ids_ref, blocks, count, offset=0):
    row_of = lax.broadcasted_iota(jnp.int32, (count, LANES), 0) + offset
    return jnp.concatenate(
        [(row_of == ids_ref[j : j + 1, :]).astype(bf16) for j in blocks], axis=1
    )


def window_offset(nodes):
    return (lax.axis_index("grid") - 1) * nodes


def gather_rows(gather_ref, dst_ref, src_ref, blocks, nodes):
    points = gather_ref.shape[1] - LANES
    lane = lax.broadcasted_iota(jnp.int32, (LANES, LANES), 1)
    for j in blocks:
        block = slice(j * LANES, (j + 1) * LANES)
        point = jnp.broadcast_to(dst_ref[j : j + 1, :], (LANES, LANES)).T
        node = jnp.broadcast_to(src_ref[j : j + 1, :], (LANES, LANES)).T
        node = node - window_offset(nodes)
        for first in range(0, points, LANES):
            gather_ref[block, first : first + LANES] = (lane + first == point).astype(bf16)
        gather_ref[block, points:] = (lane == node).astype(bf16)


def forward_kernel(
    lower_ref,
    upper_ref,
    dst_any,
    src_any,
    own_any,
    readout_any,
    bias_any,
    w_any,
    embed_any,
    forecast_ref,
    proj_ref,
    dst_ref,
    src_ref,
    own_ref,
    readout_ref,
    bias_ref,
    w_ref,
    embed_ref,
    readout_pad,
    bias_pad,
    gather_ref,
    scatter_ref,
    sources,
    message,
    in_sems,
    w_sems,
    embed_sems,
):
    channels = w_ref.shape[1]
    edges = gather_ref.shape[0]
    points = embed_ref.shape[0]
    variables = readout_ref.shape[0]
    members_nodes = own_ref.shape[0]
    window = 3 * members_nodes
    cuts = [slice(first, first + CHUNK) for first in range(0, channels, CHUNK)]
    small = started(
        [
            (dst_any, dst_ref),
            (src_any, src_ref),
            (own_any, own_ref),
            (readout_any, readout_ref),
            (bias_any, bias_ref),
        ],
        in_sems,
    )
    embeds = started([(embed_any.at[:, cut], embed_ref.at[:, cut]) for cut in cuts], embed_sems)
    weights = started([(w_any.at[:, cut], w_ref.at[:, cut]) for cut in cuts], w_sems)
    readout_pad[...] = jnp.zeros_like(readout_pad)
    bias_pad[...] = jnp.zeros_like(bias_pad)
    for slot in range(2):
        sources[slot, points + window :, :] = jnp.zeros((LANES - window, CHUNK), bf16)
    for copy in small:
        copy.wait()
    readout_pad[:variables, :] = readout_ref[...]
    bias_pad[:, :variables] = bias_ref[...]
    nodes = jnp.concatenate([lower_ref[...], own_ref[...], upper_ref[...]], axis=0)

    def build_tables(rows):
        blocks = range(rows.start // LANES, rows.stop // LANES)
        scatter_ref[:, rows] = one_hot_rows(dst_ref, blocks, points)
        gather_rows(gather_ref, dst_ref, src_ref, blocks, members_nodes)

    steps = [(n, slice(t, t + TILE)) for n in range(len(cuts)) for t in range(0, edges, TILE)]

    def preact_of(step):
        n, rows = step
        if rows.start == 0:
            embeds[n].wait()
            weights[n].wait()
            proj = jnp.dot(nodes, w_ref[:, cuts[n]], preferred_element_type=f32).astype(bf16)
            proj_ref[:, cuts[n]] = proj
            sources[n % 2, :points, :] = embed_ref[:, cuts[n]]
            sources[n % 2, points : points + window, :] = proj
        if n == 0:
            build_tables(rows)
        return jnp.dot(gather_ref[rows, :], sources[n % 2], preferred_element_type=f32)

    total = jnp.broadcast_to(bias_pad[...], forecast_ref.shape)
    following = preact_of(steps[0])
    for index, (n, rows) in enumerate(steps):
        preact = following
        if index + 1 < len(steps):
            following = preact_of(steps[index + 1])
        half = 0.5 * preact
        turn = jnp.tanh(half)
        silu = half + half * turn
        message[n % 2, rows, :] = silu.astype(bf16)
        if rows.stop == edges:
            summed = jnp.dot(scatter_ref[...], message[n % 2], preferred_element_type=f32)
            total = total + lax.dot_general(
                summed.astype(bf16),
                readout_pad[:, cuts[n]],
                (((1,), (1,)), ((), ())),
                preferred_element_type=f32,
            )
    codes = jnp.floor(jnp.log(1.0 + jnp.abs(total) * CODE_SCALE) * CODE_STEPS + 0.5)
    codes = jnp.where(total < 0.0, -codes, codes)
    forecast_ref[...] = codes.astype(jnp.int32).astype(jnp.int16)


def forward(lower, upper, dst, src, own, readout, bias, w_src, embed):
    points, channels = embed.shape
    edges = dst.size
    chunks = channels // CHUNK
    held = [(a.shape, a.dtype) for a in (dst, src, own, readout, bias, w_src, embed)]
    held += [((LANES, channels), bf16), ((1, LANES), f32)]
    held += [((edges, points + LANES), bf16), ((points, edges), bf16)]
    held += [((2, points + LANES, CHUNK), bf16), ((2, edges, CHUNK), bf16)]
    return pl.pallas_call(
        forward_kernel,
        in_specs=[VMEM] * 2 + [ANYWHERE] * 7,
        out_specs=[VMEM] * 2,
        out_shape=[
            jax.ShapeDtypeStruct((points, LANES), jnp.int16),
            jax.ShapeDtypeStruct((3 * own.shape[0], channels), bf16),
        ],
        scratch_shapes=[pltpu.VMEM(shape, kind) for shape, kind in held]
        + [pltpu.SemaphoreType.DMA((count,)) for count in (5, chunks, chunks)],
        compiler_params=grant(55350),
        cost_estimate=pl.CostEstimate(
            flops=4 * edges * points * channels, bytes_accessed=2**23, transcendentals=edges * channels
        ),
        name="forward",
    )(lower, upper, dst, src, own, readout, bias, w_src, embed)


def pair_kernel(
    variables,
    codes_ref,
    target_ref,
    weight_ref,
    after_ref,
    out_ref,
    forecasts_ref,
    grad_ref,
):
    del after_ref
    members, part, _ = codes_ref.shape
    step = 8
    for m in range(members):
        codes = codes_ref[m].astype(jnp.int32).astype(f32)
        size = (jnp.exp(jnp.abs(codes) * (1.0 / CODE_STEPS)) - 1.0) * (1.0 / CODE_SCALE)
        forecasts_ref[m] = jnp.where(codes < 0.0, -size, size)
    loss = jnp.zeros((step, LANES), f32)
    for first in range(0, part, step):
        rows = slice(first, first + step)
        fc = [forecasts_ref[m, rows, :] for m in range(members)]
        target, weight = target_ref[rows, :], weight_ref[rows, :]
        slopes = [jnp.zeros((step, LANES), f32)] * members
        pair = jnp.zeros((step, LANES), f32)
        for m in range(members):
            for k in range(m + 1, members):
                d = fc[m] - fc[k]
                s = d * d + smooth_width * smooth_width
                q = lax.rsqrt(s)
                pair = pair + (s * q - smooth_width)
                slope = d * q
                slopes[m] = slopes[m] + slope
                slopes[k] = slopes[k] - slope
        skill = jnp.zeros((step, LANES), f32)
        for m in range(members):
            d = fc[m] - target
            s = d * d + smooth_width * smooth_width
            q = lax.rsqrt(s)
            skill = skill + (s * q - smooth_width)
            slopes[m] = weight * (d * q - slopes[m] * (1.0 / (members - 1)))
        loss = loss + weight * (skill - pair * (1.0 / (members - 1)))
        for m in range(members):
            grad_ref[m, rows, :] = slopes[m]
    total = jnp.sum(loss, axis=(0, 1), keepdims=True)
    high = total.astype(bf16).astype(f32)
    middle = (total - high).astype(bf16).astype(f32)
    low = total - high - middle
    lane = lax.broadcasted_iota(jnp.int32, (step, LANES), 1)
    row = lax.broadcasted_iota(jnp.int32, (step, LANES), 0)
    note = jnp.where(lane == variables, high, 0.0)
    note = jnp.where(lane == variables + 1, middle, note)
    note = jnp.where(lane == variables + 2, low, note)
    note = jnp.where(row == 0, note, 0.0)
    spare = lane >= variables
    for m in range(members):
        grad_ref[m, :step, :] = jnp.where(spare, note, grad_ref[m, :step, :])
    out_ref[...] = grad_ref[...].astype(bf16)


def pairs(variables, forecasts, target, weight, after):
    return pl.pallas_call(
        functools.partial(pair_kernel, variables),
        in_specs=[VMEM] * 3 + [ANYWHERE],
        out_specs=VMEM,
        out_shape=jax.ShapeDtypeStruct(forecasts.shape, bf16),
        scratch_shapes=[pltpu.VMEM(forecasts.shape, f32)] * 2,
        compiler_params=grant(8192),
        cost_estimate=pl.CostEstimate(flops=2**23, bytes_accessed=2**19, transcendentals=2**19),
        name="pairs",
    )(forecasts, target, weight, after)


def slope_kernel(
    proj_ref,
    dst_ref,
    src_ref,
    readout_ref,
    embed_ref,
    slope_any,
    window_ref,
    readout_pad,
    gather_ref,
    sources,
    slope_ref,
    sems,
):
    edges, channels = slope_ref.shape
    points = embed_ref.shape[0]
    window = proj_ref.shape[0]
    blocks = range(edges // LANES)
    nodes = window // 3
    gather_rows(gather_ref, dst_ref, src_ref, blocks, nodes)
    window_ref[...] = one_hot_rows(src_ref, blocks, window, window_offset(nodes))
    readout_pad[...] = jnp.zeros_like(readout_pad)
    readout_pad[: readout_ref.shape[0], :] = readout_ref[...]
    sources[points + window :, :] = jnp.zeros((LANES - window, CHUNK), bf16)
    stores = []
    for n, first_channel in enumerate(range(0, channels, CHUNK)):
        cut = slice(first_channel, first_channel + CHUNK)
        sources[:points, :] = embed_ref[:, cut]
        sources[points : points + window, :] = proj_ref[:, cut]
        for first in range(0, edges, TILE):
            rows = slice(first, first + TILE)
            preact = jnp.dot(gather_ref[rows, :], sources[...], preferred_element_type=f32)
            half = 0.5 * preact
            turn = jnp.tanh(half)
            silu = half + half * turn
            slope = 0.5 + 0.5 * turn + silu * (0.5 - 0.5 * turn)
            slope_ref[rows, cut] = slope.astype(bf16)
        stores += started([(slope_ref.at[:, cut], slope_any.at[:, cut])], sems.at[n : n + 1])
    for copy in stores:
        copy.wait()


def slopes(proj, dst, src, readout, embed):
    points, channels = embed.shape
    edges = dst.size
    return pl.pallas_call(
        slope_kernel,
        in_specs=[VMEM] * 5,
        out_specs=[ANYWHERE, VMEM, VMEM],
        out_shape=[
            jax.ShapeDtypeStruct((edges, channels), bf16),
            jax.ShapeDtypeStruct((proj.shape[0], edges), bf16),
            jax.ShapeDtypeStruct((LANES, channels), bf16),
        ],
        scratch_shapes=[
            pltpu.VMEM((edges, points + LANES), bf16),
            pltpu.VMEM((points + LANES, CHUNK), bf16),
            pltpu.VMEM((edges, channels), bf16),
            pltpu.SemaphoreType.DMA((channels // CHUNK,)),
        ],
        compiler_params=grant(53248),
        cost_estimate=pl.CostEstimate(
            flops=2 * edges * points * channels, bytes_accessed=2**23, transcendentals=edges * channels
        ),
        name="slopes",
    )(proj, dst, src, readout, embed)


def backward_kernel(
    grad_ref,
    dst_ref,
    window_ref,
    readout_ref,
    slope_any,
    lower_ref,
    own_ref,
    upper_ref,
    slope_ref,
    sems,
):
    edges, channels = slope_ref.shape
    nodes = own_ref.shape[0]
    cuts = [slice(first, first + CHUNK) for first in range(0, channels, CHUNK)]
    loads = started([(slope_any.at[:, cut], slope_ref.at[:, cut]) for cut in cuts], sems)
    scatter = one_hot_rows(dst_ref, range(edges // LANES), grad_ref.shape[0])
    edge_grad = jnp.dot(grad_ref[...].T, scatter, preferred_element_type=f32)
    edge_grad = edge_grad.astype(bf16).T
    for n, cut in enumerate(cuts):
        loads[n].wait()
        grad_pre = []
        for first in range(0, edges, TILE):
            rows = slice(first, first + TILE)
            grad_msg = jnp.dot(edge_grad[rows], readout_ref[:, cut], preferred_element_type=f32)
            grad_msg = grad_msg.astype(bf16).astype(f32)
            grad_pre.append((grad_msg * slope_ref[rows, cut].astype(f32)).astype(bf16))
        grad_pre = jnp.concatenate(grad_pre, axis=0)
        window = jnp.dot(window_ref[...], grad_pre, preferred_element_type=f32)
        lower_ref[:, cut] = window[:nodes].astype(bf16)
        own_ref[:, cut] = window[nodes : 2 * nodes]
        upper_ref[:, cut] = window[2 * nodes :].astype(bf16)


def backward(grad_points, dst, window, readout, slope, nodes):
    edges, channels = slope.shape
    points = grad_points.shape[0]
    return pl.pallas_call(
        backward_kernel,
        in_specs=[VMEM] * 4 + [ANYWHERE],
        out_specs=[VMEM] * 3,
        out_shape=[jax.ShapeDtypeStruct((nodes, channels), kind) for kind in (bf16, f32, bf16)],
        scratch_shapes=[
            pltpu.VMEM((edges, channels), bf16),
            pltpu.SemaphoreType.DMA((channels // CHUNK,)),
        ],
        compiler_params=grant(53900),
        cost_estimate=pl.CostEstimate(
            flops=2 * edges * points * channels, bytes_accessed=2**22, transcendentals=0
        ),
        name="backward",
    )(grad_points, dst, window, readout, slope)


def note_kernel(variables, grad_ref, notes_ref):
    rows = grad_ref[:, :16, :].astype(f32)
    lane = lax.broadcasted_iota(jnp.int32, rows.shape, 2)
    row = lax.broadcasted_iota(jnp.int32, rows.shape, 1)
    kept = (row == 0) & (lane >= variables) & (lane < variables + 3)
    total = jnp.sum(jnp.sum(jnp.where(kept, rows, 0.0), axis=0), axis=(0, 1), keepdims=True)
    notes_ref[...] = jnp.broadcast_to(total[None], notes_ref.shape)


def loss_notes(variables, grad_points, copies):
    return pl.pallas_call(
        functools.partial(note_kernel, variables),
        in_specs=[VMEM],
        out_specs=VMEM,
        out_shape=jax.ShapeDtypeStruct((copies, 8, LANES), f32),
        compiler_params=grant(4096),
        name="loss_notes",
    )(grad_points)


def relay_kernel(notes_ref, below_any, out_ref, passed_any):
    del below_any, passed_any
    out_ref[...] = jnp.broadcast_to(jnp.sum(notes_ref[...], axis=0)[None], out_ref.shape)


def relay(notes, below, copies):
    return pl.pallas_call(
        relay_kernel,
        in_specs=[VMEM, ANYWHERE],
        out_specs=[VMEM, ANYWHERE],
        out_shape=[
            jax.ShapeDtypeStruct((copies,) + notes.shape[1:], f32),
            jax.ShapeDtypeStruct(below.shape, below.dtype),
        ],
        input_output_aliases={1: 1},
        compiler_params=grant(4096),
        name="relay",
    )(notes, below)


def finish_kernel(scale, own_ref, above_ref, below_ref, w_ref, notes_ref, grad_ref, loss_ref):
    total = own_ref[...] + above_ref[...].astype(f32) + below_ref[...].astype(f32)
    grad_ref[...] = lax.dot_general(
        total.astype(bf16), w_ref[...], (((1,), (1,)), ((), ())), preferred_element_type=f32
    )
    loss_ref[...] = jnp.sum(notes_ref[...], axis=0)[:1, :1] * scale


def finish(scale, own, above, below, w_src, notes):
    return pl.pallas_call(
        functools.partial(finish_kernel, scale),
        in_specs=[VMEM] * 5,
        out_specs=[VMEM] * 2,
        out_shape=[
            jax.ShapeDtypeStruct((own.shape[0], w_src.shape[0]), f32),
            jax.ShapeDtypeStruct((1, 1), f32),
        ],
        compiler_params=grant(8192),
        cost_estimate=pl.CostEstimate(flops=2**26, bytes_accessed=2**21, transcendentals=0),
        name="finish",
    )(own, above, below, w_src, notes)


def shards(
    hidden_mesh_vectors,
    grid_embed,
    w_src,
    readout_matrix,
    b_out,
    verifying_reanalysis,
    var_w,
    area_w,
    edge_src,
    edge_dst,
):
    nodes_dev = hidden_mesh_vectors.shape[1]
    points_dev = grid_embed.shape[0]
    variables = readout_matrix.shape[0]
    members = lax.axis_size("ens")
    part = points_dev // members
    lane_pad = LANES - variables
    ens_rank = lax.axis_index("ens")
    ends = lax.axis_size("grid") - 1
    upward = [(i, i + 1) for i in range(ends)]
    downward = [(i + 1, i) for i in range(ends)]

    own = hidden_mesh_vectors[0]
    lower = lax.ppermute(own, "grid", upward)
    upper = lax.ppermute(own, "grid", downward)

    src = edge_src.reshape(-1, LANES)
    dst = edge_dst.reshape(-1, LANES)
    var_weight = jnp.pad(var_w, (0, lane_pad))
    area = lax.dynamic_slice_in_dim(area_w, ens_rank * part, part, axis=0)
    target = lax.dynamic_slice_in_dim(verifying_reanalysis, ens_rank * part, part, axis=1)
    target = jnp.pad(target.T, ((0, 0), (0, lane_pad)))
    weight = area[:, None] * var_weight[None, :]

    forecast, proj = forward(
        lower, upper, dst, src, own, readout_matrix, b_out[None, :], w_src, grid_embed
    )
    forecasts = lax.all_to_all(forecast.reshape(members, part, LANES), "ens", 0, 0)
    slope, window, readout = slopes(proj, dst, src, readout_matrix, grid_embed)
    grad_members = pairs(variables, forecasts, target, weight, window)
    grad_points = lax.all_to_all(grad_members, "ens", 0, 0)

    shards_grid = lax.axis_size("grid")
    near = 8
    rows = [[first + j for j in range(near)] for first in range(0, shards_grid, near)]
    columns = [list(group) for group in zip(*rows)]
    notes = loss_notes(variables, grad_points, near)
    notes = lax.all_to_all(notes, "grid", 0, 0, axis_index_groups=rows)
    below, middle, above = backward(
        grad_points.reshape(points_dev, LANES), dst, window, readout, slope, nodes_dev
    )
    notes, below = relay(notes, below, shards_grid // near)
    notes = lax.all_to_all(notes, "grid", 0, 0, axis_index_groups=columns)
    from_above = lax.ppermute(below, "grid", downward)
    from_below = lax.ppermute(above, "grid", upward)
    scale = 1.0 / (members * variables * points_dev * shards_grid)
    grad_nodes, loss = finish(scale, middle, from_above, from_below, w_src, notes)
    return (grad_nodes[None], loss[0, 0])


def solution(mesh):
    in_specs = (
        P("ens", "grid", None),
        P("grid", None),
        P(),
        P(),
        P(),
        P(None, "grid"),
        P(),
        P("grid"),
        P("grid"),
        P("grid"),
    )
    out_specs = (P("ens", "grid", None), P())
    return jax.shard_map(shards, mesh=mesh, in_specs=in_specs, out_specs=out_specs, check_vma=False)
```

```python
import functools

import jax
import jax.numpy as jnp
from jax import lax
from jax.experimental import pallas as pl
from jax.experimental.pallas import tpu as pltpu
from jax.sharding import PartitionSpec as P

smooth_width = 0.1
LANES = 128
CHUNK = 512
TILE = 768
CODE_STEPS = 1280.0
CODE_SCALE = 64.0
f32 = jnp.float32
bf16 = jnp.bfloat16
VMEM = pl.BlockSpec(memory_space=pltpu.VMEM)
ANYWHERE = pl.BlockSpec(memory_space=pl.ANY)


def grant(kibibytes):
    return pltpu.CompilerParams(vmem_limit_bytes=kibibytes * 2**10)


def started(pairs_of_refs, sems):
    copies = [
        pltpu.make_async_copy(source, target, sems.at[index])
        for index, (source, target) in enumerate(pairs_of_refs)
    ]
    for copy in copies:
        copy.start()
    return copies


def one_hot_rows(ids_ref, blocks, count, offset=0):
    row_of = lax.broadcasted_iota(jnp.int32, (count, LANES), 0) + offset
    return jnp.concatenate(
        [(row_of == ids_ref[j : j + 1, :]).astype(bf16) for j in blocks], axis=1
    )


def window_offset(nodes):
    return (lax.axis_index("grid") - 1) * nodes


def gather_rows(gather_ref, dst_ref, src_ref, blocks, nodes):
    points = gather_ref.shape[1] - LANES
    lane = lax.broadcasted_iota(jnp.int32, (LANES, LANES), 1)
    for j in blocks:
        block = slice(j * LANES, (j + 1) * LANES)
        point = jnp.broadcast_to(dst_ref[j : j + 1, :], (LANES, LANES)).T
        node = jnp.broadcast_to(src_ref[j : j + 1, :], (LANES, LANES)).T
        node = node - window_offset(nodes)
        for first in range(0, points, LANES):
            gather_ref[block, first : first + LANES] = (lane + first == point).astype(bf16)
        gather_ref[block, points:] = (lane == node).astype(bf16)


def forward_kernel(
    lower_ref,
    upper_ref,
    dst_any,
    src_any,
    own_any,
    readout_any,
    bias_any,
    w_any,
    embed_any,
    forecast_ref,
    proj_ref,
    dst_ref,
    src_ref,
    own_ref,
    readout_ref,
    bias_ref,
    w_ref,
    embed_ref,
    readout_pad,
    bias_pad,
    gather_ref,
    scatter_ref,
    sources,
    in_sems,
    w_sems,
    embed_sems,
):
    channels = w_ref.shape[1]
    edges = gather_ref.shape[0]
    points = embed_ref.shape[0]
    variables = readout_ref.shape[0]
    members_nodes = own_ref.shape[0]
    window = 3 * members_nodes
    cuts = [slice(first, first + CHUNK) for first in range(0, channels, CHUNK)]
    small = started(
        [
            (dst_any, dst_ref),
            (src_any, src_ref),
            (own_any, own_ref),
            (readout_any, readout_ref),
            (bias_any, bias_ref),
        ],
        in_sems,
    )
    embeds = started([(embed_any.at[:, cut], embed_ref.at[:, cut]) for cut in cuts], embed_sems)
    weights = started([(w_any.at[:, cut], w_ref.at[:, cut]) for cut in cuts], w_sems)
    readout_pad[...] = jnp.zeros_like(readout_pad)
    bias_pad[...] = jnp.zeros_like(bias_pad)
    for slot in range(2):
        sources[slot, points + window :, :] = jnp.zeros((LANES - window, CHUNK), bf16)
    for copy in small:
        copy.wait()
    readout_pad[:variables, :] = readout_ref[...]
    bias_pad[:, :variables] = bias_ref[...]
    nodes = jnp.concatenate([lower_ref[...], own_ref[...], upper_ref[...]], axis=0)

    def build_tables(rows):
        blocks = range(rows.start // LANES, rows.stop // LANES)
        scatter_ref[:, rows] = one_hot_rows(dst_ref, blocks, points)
        gather_rows(gather_ref, dst_ref, src_ref, blocks, members_nodes)

    steps = [(n, slice(t, t + TILE)) for n in range(len(cuts)) for t in range(0, edges, TILE)]

    def preact_of(step):
        n, rows = step
        if rows.start == 0:
            embeds[n].wait()
            weights[n].wait()
            proj = jnp.dot(nodes, w_ref[:, cuts[n]], preferred_element_type=f32).astype(bf16)
            proj_ref[:, cuts[n]] = proj
            sources[n % 2, :points, :] = embed_ref[:, cuts[n]]
            sources[n % 2, points : points + window, :] = proj
        if n == 0:
            build_tables(rows)
        return jnp.dot(gather_ref[rows, :], sources[n % 2], preferred_element_type=f32)

    total = jnp.broadcast_to(bias_pad[...], forecast_ref.shape)
    following = preact_of(steps[0])
    for index, (n, rows) in enumerate(steps):
        preact = following
        if index + 1 < len(steps):
            following = preact_of(steps[index + 1])
        half = 0.5 * preact
        turn = jnp.tanh(half)
        silu = half + half * turn
        part = jnp.dot(scatter_ref[:, rows], silu.astype(bf16), preferred_element_type=f32)
        summed = part if rows.start == 0 else summed + part
        if rows.stop == edges:
            total = total + lax.dot_general(
                summed.astype(bf16),
                readout_pad[:, cuts[n]],
                (((1,), (1,)), ((), ())),
                preferred_element_type=f32,
            )
    codes = jnp.floor(jnp.log(1.0 + jnp.abs(total) * CODE_SCALE) * CODE_STEPS + 0.5)
    codes = jnp.where(total < 0.0, -codes, codes)
    forecast_ref[...] = codes.astype(jnp.int32).astype(jnp.int16)


def forward(lower, upper, dst, src, own, readout, bias, w_src, embed):
    points, channels = embed.shape
    edges = dst.size
    chunks = channels // CHUNK
    held = [(a.shape, a.dtype) for a in (dst, src, own, readout, bias, w_src, embed)]
    held += [((LANES, channels), bf16), ((1, LANES), f32)]
    held += [((edges, points + LANES), bf16), ((points, edges), bf16)]
    held += [((2, points + LANES, CHUNK), bf16)]
    return pl.pallas_call(
        forward_kernel,
        in_specs=[VMEM] * 2 + [ANYWHERE] * 7,
        out_specs=[VMEM] * 2,
        out_shape=[
            jax.ShapeDtypeStruct((points, LANES), jnp.int16),
            jax.ShapeDtypeStruct((3 * own.shape[0], channels), bf16),
        ],
        scratch_shapes=[pltpu.VMEM(shape, kind) for shape, kind in held]
        + [pltpu.SemaphoreType.DMA((count,)) for count in (5, chunks, chunks)],
        compiler_params=grant(55350),
        cost_estimate=pl.CostEstimate(
            flops=4 * edges * points * channels, bytes_accessed=2**23, transcendentals=edges * channels
        ),
        name="forward",
    )(lower, upper, dst, src, own, readout, bias, w_src, embed)


def pair_kernel(
    variables,
    codes_ref,
    target_ref,
    weight_ref,
    after_ref,
    out_ref,
    forecasts_ref,
    grad_ref,
):
    del after_ref
    members, part, _ = codes_ref.shape
    step = 8
    for m in range(members):
        codes = codes_ref[m].astype(jnp.int32).astype(f32)
        size = (jnp.exp(jnp.abs(codes) * (1.0 / CODE_STEPS)) - 1.0) * (1.0 / CODE_SCALE)
        forecasts_ref[m] = jnp.where(codes < 0.0, -size, size)
    loss = jnp.zeros((step, LANES), f32)
    for first in range(0, part, step):
        rows = slice(first, first + step)
        fc = [forecasts_ref[m, rows, :] for m in range(members)]
        target, weight = target_ref[rows, :], weight_ref[rows, :]
        slopes = [jnp.zeros((step, LANES), f32)] * members
        pair = jnp.zeros((step, LANES), f32)
        for m in range(members):
            for k in range(m + 1, members):
                d = fc[m] - fc[k]
                s = d * d + smooth_width * smooth_width
                q = lax.rsqrt(s)
                pair = pair + (s * q - smooth_width)
                slope = d * q
                slopes[m] = slopes[m] + slope
                slopes[k] = slopes[k] - slope
        skill = jnp.zeros((step, LANES), f32)
        for m in range(members):
            d = fc[m] - target
            s = d * d + smooth_width * smooth_width
            q = lax.rsqrt(s)
            skill = skill + (s * q - smooth_width)
            slopes[m] = weight * (d * q - slopes[m] * (1.0 / (members - 1)))
        loss = loss + weight * (skill - pair * (1.0 / (members - 1)))
        for m in range(members):
            grad_ref[m, rows, :] = slopes[m]
    total = jnp.sum(loss, axis=(0, 1), keepdims=True)
    high = total.astype(bf16).astype(f32)
    middle = (total - high).astype(bf16).astype(f32)
    low = total - high - middle
    lane = lax.broadcasted_iota(jnp.int32, (step, LANES), 1)
    row = lax.broadcasted_iota(jnp.int32, (step, LANES), 0)
    note = jnp.where(lane == variables, high, 0.0)
    note = jnp.where(lane == variables + 1, middle, note)
    note = jnp.where(lane == variables + 2, low, note)
    note = jnp.where(row == 0, note, 0.0)
    spare = lane >= variables
    for m in range(members):
        grad_ref[m, :step, :] = jnp.where(spare, note, grad_ref[m, :step, :])
    out_ref[...] = grad_ref[...].astype(bf16)


def pairs(variables, forecasts, target, weight, after):
    return pl.pallas_call(
        functools.partial(pair_kernel, variables),
        in_specs=[VMEM] * 3 + [ANYWHERE],
        out_specs=VMEM,
        out_shape=jax.ShapeDtypeStruct(forecasts.shape, bf16),
        scratch_shapes=[pltpu.VMEM(forecasts.shape, f32)] * 2,
        compiler_params=grant(8192),
        cost_estimate=pl.CostEstimate(flops=2**23, bytes_accessed=2**19, transcendentals=2**19),
        name="pairs",
    )(forecasts, target, weight, after)


def slope_kernel(
    proj_ref,
    dst_ref,
    src_ref,
    readout_ref,
    embed_ref,
    slope_any,
    window_ref,
    readout_pad,
    gather_ref,
    sources,
    slope_ref,
    sems,
):
    edges, channels = slope_ref.shape
    points = embed_ref.shape[0]
    window = proj_ref.shape[0]
    blocks = range(edges // LANES)
    nodes = window // 3
    gather_rows(gather_ref, dst_ref, src_ref, blocks, nodes)
    window_ref[...] = one_hot_rows(src_ref, blocks, window, window_offset(nodes))
    readout_pad[...] = jnp.zeros_like(readout_pad)
    readout_pad[: readout_ref.shape[0], :] = readout_ref[...]
    sources[points + window :, :] = jnp.zeros((LANES - window, CHUNK), bf16)
    stores = []
    for n, first_channel in enumerate(range(0, channels, CHUNK)):
        cut = slice(first_channel, first_channel + CHUNK)
        sources[:points, :] = embed_ref[:, cut]
        sources[points : points + window, :] = proj_ref[:, cut]
        for first in range(0, edges, TILE):
            rows = slice(first, first + TILE)
            preact = jnp.dot(gather_ref[rows, :], sources[...], preferred_element_type=f32)
            half = 0.5 * preact
            turn = jnp.tanh(half)
            silu = half + half * turn
            slope = 0.5 + 0.5 * turn + silu * (0.5 - 0.5 * turn)
            slope_ref[rows, cut] = slope.astype(bf16)
        stores += started([(slope_ref.at[:, cut], slope_any.at[:, cut])], sems.at[n : n + 1])
    for copy in stores:
        copy.wait()


def slopes(proj, dst, src, readout, embed):
    points, channels = embed.shape
    edges = dst.size
    return pl.pallas_call(
        slope_kernel,
        in_specs=[VMEM] * 5,
        out_specs=[ANYWHERE, VMEM, VMEM],
        out_shape=[
            jax.ShapeDtypeStruct((edges, channels), bf16),
            jax.ShapeDtypeStruct((proj.shape[0], edges), bf16),
            jax.ShapeDtypeStruct((LANES, channels), bf16),
        ],
        scratch_shapes=[
            pltpu.VMEM((edges, points + LANES), bf16),
            pltpu.VMEM((points + LANES, CHUNK), bf16),
            pltpu.VMEM((edges, channels), bf16),
            pltpu.SemaphoreType.DMA((channels // CHUNK,)),
        ],
        compiler_params=grant(53248),
        cost_estimate=pl.CostEstimate(
            flops=2 * edges * points * channels, bytes_accessed=2**23, transcendentals=edges * channels
        ),
        name="slopes",
    )(proj, dst, src, readout, embed)


def loss_note(variables, grad_ref, part):
    lane = lax.broadcasted_iota(jnp.int32, (16, LANES), 1)
    row = lax.broadcasted_iota(jnp.int32, (16, LANES), 0)
    kept = (row == 0) & (lane >= variables) & (lane < variables + 3)
    total = jnp.zeros((16, LANES), f32)
    for first in range(0, grad_ref.shape[0], part):
        total = total + grad_ref[first : first + 16, :].astype(f32)
    return jnp.sum(jnp.where(kept, total, 0.0), axis=(0, 1), keepdims=True)


def backward_kernel(
    variables,
    part,
    grad_ref,
    dst_ref,
    window_ref,
    readout_ref,
    slope_any,
    lower_ref,
    own_ref,
    upper_ref,
    notes_ref,
    slope_ref,
    sems,
):
    edges, channels = slope_ref.shape
    nodes = own_ref.shape[0]
    cuts = [slice(first, first + CHUNK) for first in range(0, channels, CHUNK)]
    loads = started([(slope_any.at[:, cut], slope_ref.at[:, cut]) for cut in cuts], sems)
    notes_ref[...] = jnp.broadcast_to(loss_note(variables, grad_ref, part)[None], notes_ref.shape)
    scatter = one_hot_rows(dst_ref, range(edges // LANES), grad_ref.shape[0])
    edge_grad = jnp.dot(grad_ref[...].T, scatter, preferred_element_type=f32)
    edge_grad = edge_grad.astype(bf16).T
    for n, cut in enumerate(cuts):
        loads[n].wait()
        grad_pre = []
        for first in range(0, edges, TILE):
            rows = slice(first, first + TILE)
            grad_msg = jnp.dot(edge_grad[rows], readout_ref[:, cut], preferred_element_type=f32)
            grad_msg = grad_msg.astype(bf16).astype(f32)
            grad_pre.append((grad_msg * slope_ref[rows, cut].astype(f32)).astype(bf16))
        grad_pre = jnp.concatenate(grad_pre, axis=0)
        window = jnp.dot(window_ref[...], grad_pre, preferred_element_type=f32)
        lower_ref[:, cut] = window[:nodes].astype(bf16)
        own_ref[:, cut] = window[nodes : 2 * nodes]
        upper_ref[:, cut] = window[2 * nodes :].astype(bf16)


def backward(variables, part, copies, grad_points, dst, window, readout, slope, nodes):
    edges, channels = slope.shape
    points = grad_points.shape[0]
    return pl.pallas_call(
        functools.partial(backward_kernel, variables, part),
        in_specs=[VMEM] * 4 + [ANYWHERE],
        out_specs=[VMEM] * 4,
        out_shape=[jax.ShapeDtypeStruct((nodes, channels), kind) for kind in (bf16, f32, bf16)]
        + [jax.ShapeDtypeStruct((copies, 8, LANES), f32)],
        scratch_shapes=[
            pltpu.VMEM((edges, channels), bf16),
            pltpu.SemaphoreType.DMA((channels // CHUNK,)),
        ],
        compiler_params=grant(53900),
        cost_estimate=pl.CostEstimate(
            flops=2 * edges * points * channels, bytes_accessed=2**22, transcendentals=0
        ),
        name="backward",
    )(grad_points, dst, window, readout, slope)


def finish_kernel(scale, own_ref, above_ref, below_ref, w_ref, notes_ref, grad_ref, loss_ref):
    total = own_ref[...] + above_ref[...].astype(f32) + below_ref[...].astype(f32)
    grad_ref[...] = lax.dot_general(
        total.astype(bf16), w_ref[...], (((1,), (1,)), ((), ())), preferred_element_type=f32
    )
    loss_ref[...] = jnp.sum(notes_ref[...], axis=0)[:1, :1] * scale


def finish(scale, own, above, below, w_src, notes):
    return pl.pallas_call(
        functools.partial(finish_kernel, scale),
        in_specs=[VMEM] * 5,
        out_specs=[VMEM] * 2,
        out_shape=[
            jax.ShapeDtypeStruct((own.shape[0], w_src.shape[0]), f32),
            jax.ShapeDtypeStruct((1, 1), f32),
        ],
        compiler_params=grant(8192),
        cost_estimate=pl.CostEstimate(flops=2**26, bytes_accessed=2**21, transcendentals=0),
        name="finish",
    )(own, above, below, w_src, notes)


def shards(
    hidden_mesh_vectors,
    grid_embed,
    w_src,
    readout_matrix,
    b_out,
    verifying_reanalysis,
    var_w,
    area_w,
    edge_src,
    edge_dst,
):
    nodes_dev = hidden_mesh_vectors.shape[1]
    points_dev = grid_embed.shape[0]
    variables = readout_matrix.shape[0]
    members = lax.axis_size("ens")
    part = points_dev // members
    lane_pad = LANES - variables
    ens_rank = lax.axis_index("ens")
    ends = lax.axis_size("grid") - 1
    upward = [(i, i + 1) for i in range(ends)]
    downward = [(i + 1, i) for i in range(ends)]

    own = hidden_mesh_vectors[0]
    lower = lax.ppermute(own, "grid", upward)
    upper = lax.ppermute(own, "grid", downward)

    src = edge_src.reshape(-1, LANES)
    dst = edge_dst.reshape(-1, LANES)
    var_weight = jnp.pad(var_w, (0, lane_pad))
    area = lax.dynamic_slice_in_dim(area_w, ens_rank * part, part, axis=0)
    target = lax.dynamic_slice_in_dim(verifying_reanalysis, ens_rank * part, part, axis=1)
    target = jnp.pad(target.T, ((0, 0), (0, lane_pad)))
    weight = area[:, None] * var_weight[None, :]

    forecast, proj = forward(
        lower, upper, dst, src, own, readout_matrix, b_out[None, :], w_src, grid_embed
    )
    forecasts = lax.all_to_all(forecast.reshape(members, part, LANES), "ens", 0, 0)
    slope, window, readout = slopes(proj, dst, src, readout_matrix, grid_embed)
    grad_members = pairs(variables, forecasts, target, weight, window)
    grad_points = lax.all_to_all(grad_members, "ens", 0, 0)

    shards_grid = lax.axis_size("grid")
    below, middle, above, notes = backward(
        variables,
        part,
        shards_grid,
        grad_points.reshape(points_dev, LANES),
        dst,
        window,
        readout,
        slope,
        nodes_dev,
    )
    from_above = lax.ppermute(below, "grid", downward)
    from_below = lax.ppermute(above, "grid", upward)
    notes = lax.all_to_all(notes, "grid", 0, 0)
    scale = 1.0 / (members * variables * points_dev * shards_grid)
    grad_nodes, loss = finish(scale, middle, from_above, from_below, w_src, notes)
    return (grad_nodes[None], loss[0, 0])


def solution(mesh):
    in_specs = (
        P("ens", "grid", None),
        P("grid", None),
        P(),
        P(),
        P(),
        P(None, "grid"),
        P(),
        P("grid"),
        P("grid"),
        P("grid"),
    )
    out_specs = (P("ens", "grid", None), P())
    return jax.shard_map(shards, mesh=mesh, in_specs=in_specs, out_specs=out_specs, check_vma=False)
```

```python
import functools

import jax
import jax.numpy as jnp
from jax import lax
from jax.experimental import pallas as pl
from jax.experimental.pallas import tpu as pltpu
from jax.sharding import PartitionSpec as P

smooth_width = 0.1
LANES = 128
CHUNK = 512
TILE = 512
CODE_STEPS = 1280.0
CODE_SCALE = 64.0
f32 = jnp.float32
bf16 = jnp.bfloat16
VMEM = pl.BlockSpec(memory_space=pltpu.VMEM)
ANYWHERE = pl.BlockSpec(memory_space=pl.ANY)


def grant(kibibytes):
    return pltpu.CompilerParams(vmem_limit_bytes=kibibytes * 2**10)


def started(pairs_of_refs, sems):
    copies = [
        pltpu.make_async_copy(source, target, sems.at[index])
        for index, (source, target) in enumerate(pairs_of_refs)
    ]
    for copy in copies:
        copy.start()
    return copies


def one_hot_rows(ids_ref, blocks, count, offset=0):
    row_of = lax.broadcasted_iota(jnp.int32, (count, LANES), 0) + offset
    return jnp.concatenate(
        [(row_of == ids_ref[j : j + 1, :]).astype(bf16) for j in blocks], axis=1
    )


def window_offset(nodes):
    return (lax.axis_index("grid") - 1) * nodes


def gather_rows(gather_ref, dst_ref, src_ref, blocks, nodes):
    points = gather_ref.shape[1] - LANES
    lane = lax.broadcasted_iota(jnp.int32, (LANES, LANES), 1)
    for j in blocks:
        block = slice(j * LANES, (j + 1) * LANES)
        point = jnp.broadcast_to(dst_ref[j : j + 1, :], (LANES, LANES)).T
        node = jnp.broadcast_to(src_ref[j : j + 1, :], (LANES, LANES)).T
        node = node - window_offset(nodes)
        for first in range(0, points, LANES):
            gather_ref[block, first : first + LANES] = (lane + first == point).astype(bf16)
        gather_ref[block, points:] = (lane == node).astype(bf16)


def forward_kernel(
    lower_ref,
    upper_ref,
    dst_any,
    src_any,
    own_any,
    readout_any,
    bias_any,
    w_any,
    embed_any,
    forecast_ref,
    proj_ref,
    dst_ref,
    src_ref,
    own_ref,
    readout_ref,
    bias_ref,
    w_ref,
    embed_ref,
    readout_pad,
    bias_pad,
    gather_ref,
    scatter_ref,
    sources,
    in_sems,
    w_sems,
    embed_sems,
):
    channels = w_ref.shape[1]
    edges = gather_ref.shape[0]
    points = embed_ref.shape[0]
    variables = readout_ref.shape[0]
    members_nodes = own_ref.shape[0]
    window = 3 * members_nodes
    cuts = [slice(first, first + CHUNK) for first in range(0, channels, CHUNK)]
    small = started(
        [
            (dst_any, dst_ref),
            (src_any, src_ref),
            (own_any, own_ref),
            (readout_any, readout_ref),
            (bias_any, bias_ref),
        ],
        in_sems,
    )
    embeds = started([(embed_any.at[:, cut], embed_ref.at[:, cut]) for cut in cuts], embed_sems)
    weights = started([(w_any.at[:, cut], w_ref.at[:, cut]) for cut in cuts], w_sems)
    readout_pad[...] = jnp.zeros_like(readout_pad)
    bias_pad[...] = jnp.zeros_like(bias_pad)
    for slot in range(2):
        sources[slot, points + window :, :] = jnp.zeros((LANES - window, CHUNK), bf16)
    for copy in small:
        copy.wait()
    readout_pad[:variables, :] = readout_ref[...]
    bias_pad[:, :variables] = bias_ref[...]
    nodes = jnp.concatenate([lower_ref[...], own_ref[...], upper_ref[...]], axis=0)

    def build_tables(rows):
        blocks = range(rows.start // LANES, rows.stop // LANES)
        scatter_ref[:, rows] = one_hot_rows(dst_ref, blocks, points)
        gather_rows(gather_ref, dst_ref, src_ref, blocks, members_nodes)

    steps = [(n, slice(t, t + TILE)) for n in range(len(cuts)) for t in range(0, edges, TILE)]

    def preact_of(step):
        n, rows = step
        if rows.start == 0:
            embeds[n].wait()
            weights[n].wait()
            proj = jnp.dot(nodes, w_ref[:, cuts[n]], preferred_element_type=f32).astype(bf16)
            proj_ref[:, cuts[n]] = proj
            sources[n % 2, :points, :] = embed_ref[:, cuts[n]]
            sources[n % 2, points : points + window, :] = proj
        if n == 0:
            build_tables(rows)
        return jnp.dot(gather_ref[rows, :], sources[n % 2], preferred_element_type=f32)

    total = jnp.broadcast_to(bias_pad[...], forecast_ref.shape)
    following = preact_of(steps[0])
    for index, (n, rows) in enumerate(steps):
        preact = following
        if index + 1 < len(steps):
            following = preact_of(steps[index + 1])
        half = 0.5 * preact
        turn = jnp.tanh(half)
        silu = half + half * turn
        part = jnp.dot(scatter_ref[:, rows], silu.astype(bf16), preferred_element_type=f32)
        summed = part if rows.start == 0 else summed + part
        if rows.stop == edges:
            total = total + lax.dot_general(
                summed.astype(bf16),
                readout_pad[:, cuts[n]],
                (((1,), (1,)), ((), ())),
                preferred_element_type=f32,
            )
    codes = jnp.floor(jnp.log(1.0 + jnp.abs(total) * CODE_SCALE) * CODE_STEPS + 0.5)
    codes = jnp.where(total < 0.0, -codes, codes)
    forecast_ref[...] = codes.astype(jnp.int32).astype(jnp.int16)


def forward(lower, upper, dst, src, own, readout, bias, w_src, embed):
    points, channels = embed.shape
    edges = dst.size
    chunks = channels // CHUNK
    held = [(a.shape, a.dtype) for a in (dst, src, own, readout, bias, w_src, embed)]
    held += [((LANES, channels), bf16), ((1, LANES), f32)]
    held += [((edges, points + LANES), bf16), ((points, edges), bf16)]
    held += [((2, points + LANES, CHUNK), bf16)]
    return pl.pallas_call(
        forward_kernel,
        in_specs=[VMEM] * 2 + [ANYWHERE] * 7,
        out_specs=[VMEM] * 2,
        out_shape=[
            jax.ShapeDtypeStruct((points, LANES), jnp.int16),
            jax.ShapeDtypeStruct((3 * own.shape[0], channels), bf16),
        ],
        scratch_shapes=[pltpu.VMEM(shape, kind) for shape, kind in held]
        + [pltpu.SemaphoreType.DMA((count,)) for count in (5, chunks, chunks)],
        compiler_params=grant(55350),
        cost_estimate=pl.CostEstimate(
            flops=4 * edges * points * channels, bytes_accessed=2**23, transcendentals=edges * channels
        ),
        name="forward",
    )(lower, upper, dst, src, own, readout, bias, w_src, embed)


def pair_kernel(
    variables,
    codes_ref,
    target_ref,
    weight_ref,
    after_ref,
    out_ref,
    forecasts_ref,
    grad_ref,
):
    del after_ref
    members, part, _ = codes_ref.shape
    step = 8
    for m in range(members):
        codes = codes_ref[m].astype(jnp.int32).astype(f32)
        size = (jnp.exp(jnp.abs(codes) * (1.0 / CODE_STEPS)) - 1.0) * (1.0 / CODE_SCALE)
        forecasts_ref[m] = jnp.where(codes < 0.0, -size, size)
    loss = jnp.zeros((step, LANES), f32)
    for first in range(0, part, step):
        rows = slice(first, first + step)
        fc = [forecasts_ref[m, rows, :] for m in range(members)]
        target, weight = target_ref[rows, :], weight_ref[rows, :]
        slopes = [jnp.zeros((step, LANES), f32)] * members
        pair = jnp.zeros((step, LANES), f32)
        for m in range(members):
            for k in range(m + 1, members):
                d = fc[m] - fc[k]
                s = d * d + smooth_width * smooth_width
                q = lax.rsqrt(s)
                pair = pair + (s * q - smooth_width)
                slope = d * q
                slopes[m] = slopes[m] + slope
                slopes[k] = slopes[k] - slope
        skill = jnp.zeros((step, LANES), f32)
        for m in range(members):
            d = fc[m] - target
            s = d * d + smooth_width * smooth_width
            q = lax.rsqrt(s)
            skill = skill + (s * q - smooth_width)
            slopes[m] = weight * (d * q - slopes[m] * (1.0 / (members - 1)))
        loss = loss + weight * (skill - pair * (1.0 / (members - 1)))
        for m in range(members):
            grad_ref[m, rows, :] = slopes[m]
    total = jnp.sum(loss, axis=(0, 1), keepdims=True)
    high = total.astype(bf16).astype(f32)
    middle = (total - high).astype(bf16).astype(f32)
    low = total - high - middle
    lane = lax.broadcasted_iota(jnp.int32, (step, LANES), 1)
    row = lax.broadcasted_iota(jnp.int32, (step, LANES), 0)
    note = jnp.where(lane == variables, high, 0.0)
    note = jnp.where(lane == variables + 1, middle, note)
    note = jnp.where(lane == variables + 2, low, note)
    note = jnp.where(row == 0, note, 0.0)
    spare = lane >= variables
    for m in range(members):
        grad_ref[m, :step, :] = jnp.where(spare, note, grad_ref[m, :step, :])
    out_ref[...] = grad_ref[...].astype(bf16)


def pairs(variables, forecasts, target, weight, after):
    return pl.pallas_call(
        functools.partial(pair_kernel, variables),
        in_specs=[VMEM] * 3 + [ANYWHERE],
        out_specs=VMEM,
        out_shape=jax.ShapeDtypeStruct(forecasts.shape, bf16),
        scratch_shapes=[pltpu.VMEM(forecasts.shape, f32)] * 2,
        compiler_params=grant(8192),
        cost_estimate=pl.CostEstimate(flops=2**23, bytes_accessed=2**19, transcendentals=2**19),
        name="pairs",
    )(forecasts, target, weight, after)


def slope_kernel(
    proj_ref,
    dst_ref,
    src_ref,
    readout_ref,
    embed_ref,
    slope_any,
    window_ref,
    readout_pad,
    gather_ref,
    sources,
    slope_ref,
    sems,
):
    edges, channels = slope_ref.shape
    points = embed_ref.shape[0]
    window = proj_ref.shape[0]
    blocks = range(edges // LANES)
    nodes = window // 3
    gather_rows(gather_ref, dst_ref, src_ref, blocks, nodes)
    window_ref[...] = one_hot_rows(src_ref, blocks, window, window_offset(nodes))
    readout_pad[...] = jnp.zeros_like(readout_pad)
    readout_pad[: readout_ref.shape[0], :] = readout_ref[...]
    sources[points + window :, :] = jnp.zeros((LANES - window, CHUNK), bf16)
    stores = []
    for n, first_channel in enumerate(range(0, channels, CHUNK)):
        cut = slice(first_channel, first_channel + CHUNK)
        sources[:points, :] = embed_ref[:, cut]
        sources[points : points + window, :] = proj_ref[:, cut]
        for first in range(0, edges, TILE):
            rows = slice(first, first + TILE)
            preact = jnp.dot(gather_ref[rows, :], sources[...], preferred_element_type=f32)
            half = 0.5 * preact
            turn = jnp.tanh(half)
            silu = half + half * turn
            slope = 0.5 + 0.5 * turn + silu * (0.5 - 0.5 * turn)
            slope_ref[rows, cut] = slope.astype(bf16)
        stores += started([(slope_ref.at[:, cut], slope_any.at[:, cut])], sems.at[n : n + 1])
    for copy in stores:
        copy.wait()


def slopes(proj, dst, src, readout, embed):
    points, channels = embed.shape
    edges = dst.size
    return pl.pallas_call(
        slope_kernel,
        in_specs=[VMEM] * 5,
        out_specs=[ANYWHERE, VMEM, VMEM],
        out_shape=[
            jax.ShapeDtypeStruct((edges, channels), bf16),
            jax.ShapeDtypeStruct((proj.shape[0], edges), bf16),
            jax.ShapeDtypeStruct((LANES, channels), bf16),
        ],
        scratch_shapes=[
            pltpu.VMEM((edges, points + LANES), bf16),
            pltpu.VMEM((points + LANES, CHUNK), bf16),
            pltpu.VMEM((edges, channels), bf16),
            pltpu.SemaphoreType.DMA((channels // CHUNK,)),
        ],
        compiler_params=grant(53248),
        cost_estimate=pl.CostEstimate(
            flops=2 * edges * points * channels, bytes_accessed=2**23, transcendentals=edges * channels
        ),
        name="slopes",
    )(proj, dst, src, readout, embed)


def loss_note(variables, grad_ref, part):
    lane = lax.broadcasted_iota(jnp.int32, (16, LANES), 1)
    row = lax.broadcasted_iota(jnp.int32, (16, LANES), 0)
    kept = (row == 0) & (lane >= variables) & (lane < variables + 3)
    total = jnp.zeros((16, LANES), f32)
    for first in range(0, grad_ref.shape[0], part):
        total = total + grad_ref[first : first + 16, :].astype(f32)
    return jnp.sum(jnp.where(kept, total, 0.0), axis=(0, 1), keepdims=True)


def backward_kernel(
    variables,
    part,
    grad_ref,
    dst_ref,
    window_ref,
    readout_ref,
    slope_any,
    lower_ref,
    own_ref,
    upper_ref,
    notes_ref,
    slope_ref,
    sems,
):
    edges, channels = slope_ref.shape
    nodes = own_ref.shape[0]
    cuts = [slice(first, first + CHUNK) for first in range(0, channels, CHUNK)]
    loads = started([(slope_any.at[:, cut], slope_ref.at[:, cut]) for cut in cuts], sems)
    notes_ref[...] = jnp.broadcast_to(loss_note(variables, grad_ref, part), notes_ref.shape)
    scatter = one_hot_rows(dst_ref, range(edges // LANES), grad_ref.shape[0])
    edge_grad = jnp.dot(grad_ref[...].T, scatter, preferred_element_type=f32)
    edge_grad = edge_grad.astype(bf16).T
    for n, cut in enumerate(cuts):
        loads[n].wait()
        grad_pre = []
        for first in range(0, edges, TILE):
            rows = slice(first, first + TILE)
            grad_msg = jnp.dot(edge_grad[rows], readout_ref[:, cut], preferred_element_type=f32)
            grad_msg = grad_msg.astype(bf16).astype(f32)
            grad_pre.append((grad_msg * slope_ref[rows, cut].astype(f32)).astype(bf16))
        grad_pre = jnp.concatenate(grad_pre, axis=0)
        window = jnp.dot(window_ref[...], grad_pre, preferred_element_type=f32)
        lower_ref[:, cut] = window[:nodes].astype(bf16)
        own_ref[:, cut] = window[nodes : 2 * nodes]
        upper_ref[:, cut] = window[2 * nodes :].astype(bf16)


def backward(variables, part, grad_points, dst, window, readout, slope, nodes):
    edges, channels = slope.shape
    points = grad_points.shape[0]
    return pl.pallas_call(
        functools.partial(backward_kernel, variables, part),
        in_specs=[VMEM] * 4 + [ANYWHERE],
        out_specs=[VMEM] * 4,
        out_shape=[jax.ShapeDtypeStruct((nodes, channels), kind) for kind in (bf16, f32, bf16)]
        + [jax.ShapeDtypeStruct((8, LANES), f32)],
        scratch_shapes=[
            pltpu.VMEM((edges, channels), bf16),
            pltpu.SemaphoreType.DMA((channels // CHUNK,)),
        ],
        compiler_params=grant(53900),
        cost_estimate=pl.CostEstimate(
            flops=2 * edges * points * channels, bytes_accessed=2**22, transcendentals=0
        ),
        name="backward",
    )(grad_points, dst, window, readout, slope)


def spread_kernel(note_ref, above_ref, below_ref, notes_ref):
    del above_ref, below_ref
    notes_ref[...] = jnp.broadcast_to(note_ref[...][None], notes_ref.shape)


def spread(note, above, below, copies):
    return pl.pallas_call(
        spread_kernel,
        in_specs=[VMEM, ANYWHERE, ANYWHERE],
        out_specs=VMEM,
        out_shape=jax.ShapeDtypeStruct((copies,) + note.shape, f32),
        compiler_params=grant(4096),
        name="spread",
    )(note, above, below)


def loss_kernel(scale, notes_ref, loss_ref):
    loss_ref[...] = jnp.sum(notes_ref[...], axis=0)[:1, :1] * scale


def loss_of(scale, notes):
    return pl.pallas_call(
        functools.partial(loss_kernel, scale),
        in_specs=[VMEM],
        out_specs=VMEM,
        out_shape=jax.ShapeDtypeStruct((1, 1), f32),
        compiler_params=grant(4096),
        name="loss_of",
    )(notes)


def finish_kernel(own_ref, above_ref, below_ref, w_ref, grad_ref):
    total = own_ref[...] + above_ref[...].astype(f32) + below_ref[...].astype(f32)
    grad_ref[...] = lax.dot_general(
        total.astype(bf16), w_ref[...], (((1,), (1,)), ((), ())), preferred_element_type=f32
    )


def finish(own, above, below, w_src):
    return pl.pallas_call(
        finish_kernel,
        in_specs=[VMEM] * 4,
        out_specs=VMEM,
        out_shape=jax.ShapeDtypeStruct((own.shape[0], w_src.shape[0]), f32),
        compiler_params=grant(8192),
        cost_estimate=pl.CostEstimate(flops=2**26, bytes_accessed=2**21, transcendentals=0),
        name="finish",
    )(own, above, below, w_src)


def shards(
    hidden_mesh_vectors,
    grid_embed,
    w_src,
    readout_matrix,
    b_out,
    verifying_reanalysis,
    var_w,
    area_w,
    edge_src,
    edge_dst,
):
    nodes_dev = hidden_mesh_vectors.shape[1]
    points_dev = grid_embed.shape[0]
    variables = readout_matrix.shape[0]
    members = lax.axis_size("ens")
    part = points_dev // members
    lane_pad = LANES - variables
    ens_rank = lax.axis_index("ens")
    ends = lax.axis_size("grid") - 1
    upward = [(i, i + 1) for i in range(ends)]
    downward = [(i + 1, i) for i in range(ends)]

    own = hidden_mesh_vectors[0]
    lower = lax.ppermute(own, "grid", upward)
    upper = lax.ppermute(own, "grid", downward)

    src = edge_src.reshape(-1, LANES)
    dst = edge_dst.reshape(-1, LANES)
    var_weight = jnp.pad(var_w, (0, lane_pad))
    area = lax.dynamic_slice_in_dim(area_w, ens_rank * part, part, axis=0)
    target = lax.dynamic_slice_in_dim(verifying_reanalysis, ens_rank * part, part, axis=1)
    target = jnp.pad(target.T, ((0, 0), (0, lane_pad)))
    weight = area[:, None] * var_weight[None, :]

    forecast, proj = forward(
        lower, upper, dst, src, own, readout_matrix, b_out[None, :], w_src, grid_embed
    )
    forecasts = lax.all_to_all(forecast.reshape(members, part, LANES), "ens", 0, 0)
    slope, window, readout = slopes(proj, dst, src, readout_matrix, grid_embed)
    grad_members = pairs(variables, forecasts, target, weight, window)
    grad_points = lax.all_to_all(grad_members, "ens", 0, 0)

    shards_grid = lax.axis_size("grid")
    below, middle, above, notes = backward(
        variables,
        part,
        grad_points.reshape(points_dev, LANES),
        dst,
        window,
        readout,
        slope,
        nodes_dev,
    )
    from_above = lax.ppermute(below, "grid", downward)
    from_below = lax.ppermute(above, "grid", upward)
    notes = lax.all_to_all(spread(notes, from_above, from_below, shards_grid), "grid", 0, 0)
    scale = 1.0 / (members * variables * points_dev * shards_grid)
    grad_nodes = finish(middle, from_above, from_below, w_src)
    loss = loss_of(scale, notes)
    return (grad_nodes[None], loss[0, 0])


def solution(mesh):
    in_specs = (
        P("ens", "grid", None),
        P("grid", None),
        P(),
        P(),
        P(),
        P(None, "grid"),
        P(),
        P("grid"),
        P("grid"),
        P("grid"),
    )
    out_specs = (P("ens", "grid", None), P())
    return jax.shard_map(shards, mesh=mesh, in_specs=in_specs, out_specs=out_specs, check_vma=False)
```
